512 devices in a mesh: width: 16 (over y, z_hi), hidden: 32 (over x, z_lo, core).
Axes of the slice: x: 4, y: 4, z: 16 (z_hi: 4, z_lo: 4; z = z_hi * 4 + z_lo), core: 2. Of those that a mesh axis runs over, the one named last changes fastest.
Arguments:
- tokens: bfloat16 [384, 12288], P('hidden', 'width'), may hold values from -8 to 8
- gate_weight: bfloat16 [12288, 28672], P('width', 'hidden'), may hold values from -0.0546875 to 0.0546875
- up_weight: bfloat16 [12288, 28672], P('width', 'hidden'), may hold values from -0.0546875 to 0.0546875
- down_weight: bfloat16 [28672, 12288], P('hidden', 'width'), may hold values from -0.03125 to 0.03125
Outputs:
- block_out: bfloat16 [384, 12288], P('hidden', 'width')
The draws below stay inside these ranges and needn't reach their ends.
All inputs are finite; a program needn't handle non-finite values.
Results may differ from the reference program's by a relative error of at most 0.0036.
Values may be sent and summed in bfloat16 or wider, within the bound.
A program may use at most 64 MiB of HBM per device.

```python
import math
import jax
import jax.numpy as jnp

D = 12288
FF = 28672
TOKENS = 384


def draw_tokens(key, part):
    key = jax.random.fold_in(key, 11)
    first, second, third, fourth, fifth, sixth, seventh = jax.random.split(key, 7)
    base = 0.6 * jax.random.normal(first, (TOKENS, D), jnp.float32)
    rows = jnp.exp(jax.random.uniform(second, (TOKENS, 1), jnp.float32, math.log(0.3), math.log(3.0)))
    cols = jnp.exp(jax.random.uniform(third, (1, D), jnp.float32, math.log(0.5), math.log(2.0)))
    drawn = jnp.clip(base * rows * cols, -2.5, 2.5)
    spot_row = jax.random.randint(fourth, (), 0, TOKENS)
    spot_col = jax.random.randint(fifth, (), 0, D)
    size = jax.random.uniform(sixth, (), jnp.float32, 4.0, 8.0)
    sign = 2.0 * jax.random.randint(seventh, (), 0, 2).astype(jnp.float32) - 1.0
    row_ids = jnp.arange(TOKENS, dtype=jnp.int32)[:, None]
    col_ids = jnp.arange(D, dtype=jnp.int32)[None, :]
    planted = (row_ids == spot_row) & (col_ids == spot_col)
    return jnp.where(planted, sign * size, drawn).astype(jnp.bfloat16)


def levels(key, dims, shards, low, high):
    loudness, own = 1.0, jax.random.fold_in(key, 6)
    for axis_at, blocks in shards:
        draws = jnp.exp(jax.random.uniform(jax.random.fold_in(own, axis_at), (blocks,), jnp.float32, low / len(shards), high / len(shards)))
        loudness = loudness * jnp.repeat(draws, dims[axis_at] // blocks).reshape([-1 if axis == axis_at else 1 for axis in range(len(dims))])
    return loudness


def noise(stream_key, extent, deviation, limit, pieces=(), held_as=jnp.bfloat16):
    array = jax.random.normal(stream_key, extent, jnp.float32) * deviation
    if len(pieces) > 0:
        array = levels(stream_key, extent, pieces, -0.22, 0.18) * array
    return jnp.clip(array, min=-limit, max=limit).astype(held_as)


def setup_inputs(seed: int = 0) -> dict:
    seeds = jax.random.split(jax.random.key(seed), 5)
    return {
        "tokens": draw_tokens(jax.random.fold_in(seeds[4], 71), 0),
        "gate_weight": noise(seeds[1], (D, FF), D ** -0.5, 0.0546875, ((0, 16), (1, 32))),
        "up_weight": noise(seeds[2], (D, FF), D ** -0.5, 0.0546875, ((0, 16), (1, 32))),
        "down_weight": noise(seeds[3], (FF, D), FF ** -0.5, 0.03125, ((0, 32), (1, 16))),
    }


def saturate(values, peak):
    level = 0.5 * (peak + 1e-6)
    return level * jnp.tanh(values / level)


def reference(tokens, gate_weight, up_weight, down_weight):
    inputs = tokens.astype(jnp.float32)
    peak_in = jnp.max(jnp.abs(inputs))
    scaled_in = saturate(inputs, peak_in).astype(jnp.bfloat16)
    gate = jnp.dot(scaled_in, gate_weight, preferred_element_type=jnp.float32)
    up = jnp.dot(scaled_in, up_weight, preferred_element_type=jnp.float32)
    act = jax.nn.silu(gate) * up
    peak_act = jnp.max(jnp.abs(act))
    scaled_act = saturate(act, 0.125 * peak_act).astype(jnp.bfloat16)
    down = jnp.dot(scaled_act, down_weight, preferred_element_type=jnp.float32)
    return (inputs + down).astype(jnp.bfloat16)
```

```python
import jax
import jax.numpy as jnp
from jax import lax
from jax.experimental import pallas as pl
from jax.experimental.pallas import tpu as pltpu
from jax.sharding import PartitionSpec as P

F32 = jnp.float32
BF16 = jnp.bfloat16

PIECES = ((0, 2), (2, 2), (4, 2), (6, 1))
MAX_COPIES = 192


def ring_add(offset, value):
    return lax.rem(value + offset, 4)


def fold_max(values):
    rows, columns = values.shape
    total = None
    for row in range(0, rows, 8):
        for column in range(0, columns, 128):
            tile = jnp.abs(values[row : row + 8, column : column + 128])
            total = tile if total is None else jnp.maximum(total, tile)
    return total


def levels(tile, factor):
    peak = jnp.max(jnp.max(tile, axis=1, keepdims=True), axis=0, keepdims=True)
    level = 0.5 * (factor * peak + 1e-06)
    return level, 1.0 / level


def kernel(
    tokens, gate_hbm, up_hbm, down_hbm, out,
    gate_w, up_w, down_w, token_pad, token_z, token_f, token_x, scaled,
    keep, y_send, y_recv, z_sum, z_sum1, z_send, z_recv, act, act1, scaled_act,
    down_part, core_send, core_recv, x_send, x_recv, l_own, l_send, l_recv,
    peak_send, peak_recv, send_sem, recv_sem, load_sem,
):
    width, hidden = lax.axis_index("width"), lax.axis_index("hidden")
    y, zh = lax.div(width, 4), lax.rem(width, 4)
    core = lax.rem(hidden, 2)
    x, zl = lax.div(hidden, 8), lax.rem(lax.div(hidden, 2), 4)
    other = 1 - core

    def device(y_=None, zh_=None, x_=None, zl_=None, core_=None):
        y_ = y if y_ is None else y_
        zh_ = zh if zh_ is None else zh_
        x_ = x if x_ is None else x_
        zl_ = zl if zl_ is None else zl_
        core_ = core if core_ is None else core_
        return (y_ * 4 + zh_, (x_ * 4 + zl_) * 2 + core_)

    def along(axis, offset):
        if axis == "y":
            return device(y_=ring_add(offset, y))
        if axis == "zh":
            return device(zh_=ring_add(offset, zh))
        if axis == "x":
            return device(x_=ring_add(offset, x))
        if axis == "zl":
            return device(zl_=ring_add(offset, zl))
        return device(core_=other)

    copies = []

    def send(source, target, to):
        at = len(copies)
        copy = pltpu.make_async_remote_copy(
            src_ref=source, dst_ref=target,
            send_sem=send_sem.at[at], recv_sem=recv_sem.at[at],
            device_id=to, device_id_type=pl.DeviceIdType.MESH,
        )
        copies.append(copy)
        copy.start()
        return copy

    loads = []
    for at, (source, target) in enumerate(
        ((gate_hbm, gate_w), (up_hbm, up_w), (down_hbm, down_w))
    ):
        load = pltpu.make_async_copy(source, target, load_sem.at[at])
        load.start()
        loads.append(load)

    partners = [along(axis, offset) for axis in ("y", "zh", "x", "zl") for offset in (1, 2, 3)]
    partners.append(along("core", 1))
    barrier = pltpu.get_barrier_semaphore()
    for partner in partners:
        pl.semaphore_signal(barrier, inc=1, device_id=partner, device_id_type=pl.DeviceIdType.MESH)
    pl.semaphore_wait(barrier, len(partners))

    def peak_start(stage, axis, tile):
        peak_send[stage] = tile
        offsets = (1,) if axis == "core" else (1, 2, 3)
        return [
            send(peak_send.at[stage], peak_recv.at[stage, offset], along(axis, offset))
            for offset in offsets
        ]

    def peak_end(stage, sent, tile):
        for copy in sent:
            copy.wait_recv()
        for offset in range(1, len(sent) + 1):
            tile = jnp.maximum(tile, peak_recv[stage, offset])
        return tile

    token_pad[0:12, :] = tokens[...].astype(F32)
    token_pad[12:16, :] = jnp.zeros((4, 768), F32)
    padded = token_pad[...]
    token_z[zl] = padded.astype(BF16)
    zl_sent = [send(token_z.at[zl], token_z.at[zl], along("zl", o)) for o in (1, 2, 3)]
    tile = fold_max(padded)
    peak_sent = peak_start(0, "y", tile)
    tile = peak_end(0, peak_sent, tile)
    peak_sent = peak_start(1, "zh", tile)
    for copy in zl_sent:
        copy.wait_recv()
    for i in range(4):
        token_f[12 * i : 12 * i + 12, :] = token_z[i].astype(F32)[0:12, :]
    token_x[x, core] = token_f[...].astype(BF16)
    mine = token_x.at[x, core]
    to_right = send(mine, mine, along("x", 1))
    to_left = send(mine, mine, along("x", 3))
    core_sent = [send(mine, mine, along("core", 1))]
    tile = peak_end(1, peak_sent, tile)
    peak_sent = peak_start(2, "zl", tile)
    tile = peak_end(2, peak_sent, tile)
    peak_sent = peak_start(3, "core", tile)
    to_right.wait_recv()
    block = token_x.at[ring_add(3, x), core]
    part = block.at[:, 0:384]
    far = [send(part, part, along("x", 1))]
    core_sent.append(send(block, block, along("core", 1)))
    to_left.wait_recv()
    block = token_x.at[ring_add(1, x), core]
    part = block.at[:, 384:768]
    far.append(send(part, part, along("x", 3)))
    core_sent.append(send(block, block, along("core", 1)))
    tile = peak_end(3, peak_sent, tile)
    peak_sent = peak_start(4, "x", tile)
    for copy in far:
        copy.wait_recv()
    block = token_x.at[ring_add(2, x), core]
    core_sent.append(send(block, block, along("core", 1)))
    tile = peak_end(4, peak_sent, tile)
    level, inverse = levels(tile, 1.0)
    for copy in core_sent:
        copy.wait_recv()
    for j in range(4):
        for c in range(2):
            values = token_x[ring_add(j, y), c].astype(F32)
            row = 96 * j + 48 * c
            scaled[row : row + 48, :] = (level * jnp.tanh(values * inverse)).astype(BF16)

    loads[0].wait()
    loads[1].wait()

    state = [dict() for _ in PIECES]

    def ring_first(axis, sends, receives):
        ends = (along(axis, 1), along(axis, 3))
        return [send(sends(m), receives(m), ends[m % 2]) for m in range(4)]

    def ring_second(axis, m, sends, receives):
        return send(sends(m), receives(m), along(axis, 1 if m == 4 else 3))

    def quarter(k, q):
        if PIECES[k][1] == 2:
            return lax.rem(q, 2), pl.multiple_of(lax.div(q, 2) * 48, 48), 48
        return 0, pl.multiple_of(q * 32, 32), 32

    def multiply(k):
        first, count = PIECES[k]
        columns = slice(128 * first, 128 * (first + count))
        gate = jnp.dot(scaled[...], gate_w[:, columns], preferred_element_type=F32)
        for t in range(count):
            lanes = slice(128 * t, 128 * t + 128)
            y_send[0, first + t] = gate[192:288, lanes].astype(BF16)
            y_send[3, first + t] = gate[288:384, lanes].astype(BF16)
            keep[0, first + t] = gate[0:96, lanes]
            keep[1, first + t] = gate[96:192, lanes]
        up = jnp.dot(scaled[...], up_w[:, columns], preferred_element_type=F32)
        for t in range(count):
            lanes = slice(128 * t, 128 * t + 128)
            y_send[1, first + t] = up[192:288, lanes].astype(BF16)
            y_send[2, first + t] = up[96:192, lanes].astype(BF16)
            keep[2, first + t] = up[0:96, lanes]
            keep[3, first + t] = up[288:384, lanes]
        state[k]["y"] = ring_first(
            "y",
            lambda m: y_send.at[m, pl.ds(first, count)],
            lambda m: y_recv.at[m, pl.ds(first, count)],
        )

    def y_second(k):
        first, count = PIECES[k]
        for m, source, own in ((4, 0, 1), (5, 1, 3)):
            state[k]["y"][source].wait_recv()
            for t in range(first, first + count):
                y_send[m, t] = (keep[own, t] + y_recv[source, t].astype(F32)).astype(BF16)
            state[k]["y"].append(
                ring_second(
                    "y", m,
                    lambda m: y_send.at[m, pl.ds(first, count)],
                    lambda m: y_recv.at[m, pl.ds(first, count)],
                )
            )

    def z_read(k, g, q):
        tile_at, row, rows = quarter(k, q)
        if PIECES[k][1] == 2:
            return z_sum[k, g, tile_at, pl.ds(row, rows), :]
        return z_sum1[g, pl.ds(row, rows), :]

    def z_ref(ref, k, m):
        return ref.at[k, m, pl.ds(0, quarter(k, 0)[2])]

    def z_rows(k):
        return quarter(k, 0)[2]

    def y_third(k):
        first, count = PIECES[k]
        for m in (2, 3, 4, 5):
            state[k]["y"][m].wait_recv()
        for t in range(count):
            for g, own, one, two in ((0, 0, 3, 4), (1, 2, 2, 5)):
                total = (
                    keep[own, first + t]
                    + y_recv[one, first + t].astype(F32)
                    + y_recv[two, first + t].astype(F32)
                )
                if count == 2:
                    z_sum[k, g, t] = total
                else:
                    z_sum1[g, 0:96, :] = total
        if count == 1:
            z_sum1[:, 96:128, :] = jnp.zeros((2, 32, 128), F32)
        for m, g, j in ((0, 0, 2), (1, 1, 2), (2, 1, 1), (3, 0, 3)):
            z_send[k, m, 0 : z_rows(k), :] = z_read(k, g, ring_add(j, zh)).astype(BF16)
        state[k]["z"] = ring_first(
            "zh", lambda m: z_ref(z_send, k, m), lambda m: z_ref(z_recv, k, m)
        )

    def z_second(k):
        rows = z_rows(k)
        for m, source, g, j in ((4, 0, 0, 1), (5, 1, 1, 3)):
            state[k]["z"][source].wait_recv()
            own = z_read(k, g, ring_add(j, zh))
            z_send[k, m, 0:rows, :] = (own + z_recv[k, source, 0:rows, :].astype(F32)).astype(BF16)
            state[k]["z"].append(
                ring_second(
                    "zh", m, lambda m: z_ref(z_send, k, m), lambda m: z_ref(z_recv, k, m)
                )
            )

    def act_ref(k, owner_y, q, low, high):
        tile_at, row, _ = quarter(k, q)
        if PIECES[k][1] == 2:
            start = pl.multiple_of(owner_y * 96 + row + low, 16)
            return act.at[PIECES[k][0] + tile_at, pl.ds(start, high - low), :]
        return act1.at[owner_y, pl.ds(pl.multiple_of(row + low, 16), high - low), :]

    peaks = []

    def z_third(k):
        rows = z_rows(k)
        for m in (2, 3, 4, 5):
            state[k]["z"][m].wait_recv()
        gate, up = (
            z_read(k, g, zh)
            + z_recv[k, one, 0:rows, :].astype(F32)
            + z_recv[k, two, 0:rows, :].astype(F32)
            for g, one, two in ((0, 3, 4), (1, 2, 5))
        )
        value = gate / (1.0 + jnp.exp(-gate)) * up
        peaks.append(fold_max(value))
        mine = act_ref(k, y, zh, 0, rows)
        mine[...] = value.astype(BF16)
        state[k]["az"] = [send(mine, mine, along("zh", 1)), send(mine, mine, along("zh", 3))]

    def act_z_second(k):
        rows = z_rows(k)
        cut = 16 if rows == 32 or k % 2 else 32
        state[k]["az"][0].wait_recv()
        part = act_ref(k, y, ring_add(3, zh), 0, cut)
        far = [send(part, part, along("zh", 1))]
        state[k]["az"][1].wait_recv()
        part = act_ref(k, y, ring_add(1, zh), cut, rows)
        far.append(send(part, part, along("zh", 3)))
        state[k]["far"] = far

    def act_rows(k, owner_y, half=None):
        first, count = PIECES[k]
        if count == 2:
            rows = pl.ds(pl.multiple_of(owner_y * 96, 96), 96)
            if half is None:
                return act.at[pl.ds(first, 2), rows, :]
            return act.at[first + half, rows, :]
        if half is None:
            return act1.at[owner_y, pl.ds(0, 96), :]
        return act1.at[owner_y, pl.ds(48 * half, 48), :]

    def act_z_third(k):
        for copy in state[k]["far"]:
            copy.wait_recv()
        mine = act_rows(k, y)
        state[k]["ay"] = [send(mine, mine, along("y", 1)), send(mine, mine, along("y", 3))]

    def act_y_second(k):
        state[k]["ay"][0].wait_recv()
        part = act_rows(k, ring_add(3, y), 0)
        far = [send(part, part, along("y", 1))]
        state[k]["ay"][1].wait_recv()
        part = act_rows(k, ring_add(1, y), 1)
        far.append(send(part, part, along("y", 3)))
        state[k]["far"] = far

    def act_y_third(k):
        for copy in state[k]["far"]:
            copy.wait_recv()

    steps = (
        multiply, y_second, y_third, z_second, z_third,
        act_z_second, act_z_third, act_y_second, act_y_third,
    )
    order = ("core", "zl", "x", "zh", "y")
    last = len(PIECES) - 1
    peak_tile, peak_sent, stage = None, None, 0
    for time in range(len(steps) + last):
        for at in range(len(steps)):
            k = time - at
            if 0 <= k <= last:
                steps[at](k)
        if time >= last + 4 and stage < len(order):
            if stage == 0:
                peak_tile = peaks[0]
                for tile in peaks[1:]:
                    peak_tile = jnp.maximum(peak_tile, tile)
            else:
                peak_tile = peak_end(4 + stage, peak_sent, peak_tile)
            peak_sent = peak_start(5 + stage, order[stage], peak_tile)
            stage += 1
    peak_tile = peak_end(9, peak_sent, peak_tile)
    level, inverse = levels(peak_tile, 0.125)

    def saturated(values):
        return (level * jnp.tanh(values.astype(F32) * inverse)).astype(BF16)

    for t in range(6):
        scaled_act[:, 128 * t : 128 * t + 128] = saturated(act[t])
    for d in range(4):
        scaled_act[96 * d : 96 * d + 96, 768:896] = saturated(act1[d, 0:96, :])

    loads[2].wait()

    downs = [dict() for _ in range(3)]

    def down_multiply(n):
        result = jnp.dot(
            scaled_act[...], down_w[:, 256 * n : 256 * n + 256], preferred_element_type=F32
        )
        for half in range(2):
            for d in range(4):
                for c in range(2):
                    row = 96 * d + 48 * c
                    down_part[n, half, c, d] = result[row : row + 48, 128 * half : 128 * half + 128]
        core_send[n] = down_part[n, :, other].astype(BF16)
        downs[n]["core"] = send(core_send.at[n], core_recv.at[n], along("core", 1))

    def down_read(n, half, j):
        d = ring_add(j, x)
        return down_part[n, half, core, d] + core_recv[n, half, d].astype(F32)

    def down_x_first(n):
        downs[n]["core"].wait_recv()
        for m, half, j in ((0, 0, 2), (1, 1, 2), (2, 1, 1), (3, 0, 3)):
            x_send[n, m] = down_read(n, half, j).astype(BF16)
        downs[n]["x"] = ring_first("x", lambda m: x_send.at[n, m], lambda m: x_recv.at[n, m])

    def down_x_second(n):
        for m, source, half, j in ((4, 0, 0, 1), (5, 1, 1, 3)):
            downs[n]["x"][source].wait_recv()
            x_send[n, m] = (down_read(n, half, j) + x_recv[n, source].astype(F32)).astype(BF16)
            downs[n]["x"].append(
                ring_second("x", m, lambda m: x_send.at[n, m], lambda m: x_recv.at[n, m])
            )

    def down_x_third(n):
        for m in (2, 3, 4, 5):
            downs[n]["x"][m].wait_recv()
        for half, one, two in ((0, 3, 4), (1, 2, 5)):
            total = (
                down_read(n, half, 0)
                + x_recv[n, one].astype(F32)
                + x_recv[n, two].astype(F32)
            )
            for i in range(4):
                rows = total if i == 0 else pltpu.roll(total, 48 - 12 * i, 0)
                l_own[n, i, half] = rows[0:16, :]
                l_send[n, i, half] = rows[0:16, :].astype(BF16)
        downs[n]["l"] = [
            send(l_send.at[n, ring_add(o, zl)], l_recv.at[n, o], along("zl", o)) for o in (1, 2, 3)
        ]

    def down_last(n):
        for copy in downs[n]["l"]:
            copy.wait_recv()
        for half in range(2):
            total = l_own[n, zl, half]
            for o in (1, 2, 3):
                total = total + l_recv[n, o, half].astype(F32)
            lanes = slice(256 * n + 128 * half, 256 * n + 128 * half + 128)
            out[:, lanes] = (token_pad[0:12, lanes] + total[0:12, :]).astype(BF16)

    down_steps = (down_multiply, down_x_first, down_x_second, down_x_third, down_last)
    for time in range(len(down_steps) + 2):
        for at in range(len(down_steps)):
            n = time - at
            if 0 <= n < 3:
                down_steps[at](n)

    for copy in copies:
        copy.wait_send()


def on_device(tokens, gate_weight, up_weight, down_weight):
    vmem = pltpu.VMEM
    return pl.pallas_call(
        kernel,
        out_shape=jax.ShapeDtypeStruct((12, 768), BF16),
        in_specs=[pl.BlockSpec(memory_space=pltpu.VMEM)]
        + [pl.BlockSpec(memory_space=pl.ANY)] * 3,
        out_specs=pl.BlockSpec(memory_space=pltpu.VMEM),
        scratch_shapes=[
            vmem((768, 896), BF16),
            vmem((768, 896), BF16),
            vmem((896, 768), BF16),
            vmem((16, 768), F32),
            vmem((4, 16, 768), BF16),
            vmem((48, 768), F32),
            vmem((4, 2, 48, 768), BF16),
            vmem((384, 768), BF16),
            vmem((4, 7, 96, 128), F32),
            vmem((6, 7, 96, 128), BF16),
            vmem((6, 7, 96, 128), BF16),
            vmem((3, 2, 2, 96, 128), F32),
            vmem((2, 128, 128), F32),
            vmem((4, 6, 48, 128), BF16),
            vmem((4, 6, 48, 128), BF16),
            vmem((6, 384, 128), BF16),
            vmem((4, 128, 128), BF16),
            vmem((384, 896), BF16),
            vmem((3, 2, 2, 4, 48, 128), F32),
            vmem((3, 2, 4, 48, 128), BF16),
            vmem((3, 2, 4, 48, 128), BF16),
            vmem((3, 6, 48, 128), BF16),
            vmem((3, 6, 48, 128), BF16),
            vmem((3, 4, 2, 16, 128), F32),
            vmem((3, 4, 2, 16, 128), BF16),
            vmem((3, 4, 2, 16, 128), BF16),
            vmem((10, 8, 128), F32),
            vmem((10, 4, 8, 128), F32),
            pltpu.SemaphoreType.DMA((MAX_COPIES,)),
            pltpu.SemaphoreType.DMA((MAX_COPIES,)),
            pltpu.SemaphoreType.DMA((3,)),
        ],
        compiler_params=pltpu.CompilerParams(
            collective_id=0, has_side_effects=True, vmem_limit_bytes=40 * 1024 * 1024
        ),
        cost_estimate=pl.CostEstimate(
            flops=6 * 384 * 768 * 896, bytes_accessed=3 * 2 * 768 * 896, transcendentals=1000000
        ),
        name="swiglu_block",
    )(tokens, gate_weight, up_weight, down_weight)


def solution(mesh):
    in_specs = (
        P("hidden", "width"),
        P("width", "hidden"),
        P("width", "hidden"),
        P("hidden", "width"),
    )
    return jax.shard_map(
        on_device, mesh=mesh, in_specs=in_specs, out_specs=P("hidden", "width"), check_vma=False
    )
```

```python
import jax
import jax.numpy as jnp
from jax import lax
from jax.experimental import pallas as pl
from jax.experimental.pallas import tpu as pltpu
from jax.sharding import PartitionSpec as P

F32 = jnp.float32
BF16 = jnp.bfloat16

PIECES = ((0, 2), (2, 2), (4, 2), (6, 1))
MAX_COPIES = 256


def ring_add(offset, value):
    return lax.rem(value + offset, 4)


def fold_max(values):
    rows, columns = values.shape
    total = None
    for row in range(0, rows, 8):
        for column in range(0, columns, 128):
            tile = jnp.abs(values[row : row + 8, column : column + 128])
            total = tile if total is None else jnp.maximum(total, tile)
    return total


def levels(tile, factor):
    peak = jnp.max(jnp.max(tile, axis=1, keepdims=True), axis=0, keepdims=True)
    level = 0.5 * (factor * peak + 1e-06)
    return level, 1.0 / level


def kernel(
    tokens, gate_hbm, up_hbm, down_hbm, out,
    gate_w, up_w, down_w, token_in, token_pad, token_z, token_f, token_x, scaled,
    keep, y_send, y_recv, z_sum, z_sum1, z_send, z_recv, act, act1, scaled_act,
    down_part, core_send, core_recv, x_send, x_recv, l_own, l_send, l_recv,
    peak_send, peak_recv, send_sem, recv_sem, load_sem,
):
    width, hidden = lax.axis_index("width"), lax.axis_index("hidden")
    y, zh = lax.div(width, 4), lax.rem(width, 4)
    core = lax.rem(hidden, 2)
    x, zl = lax.div(hidden, 8), lax.rem(lax.div(hidden, 2), 4)
    other = 1 - core

    def device(y_=None, zh_=None, x_=None, zl_=None, core_=None):
        y_ = y if y_ is None else y_
        zh_ = zh if zh_ is None else zh_
        x_ = x if x_ is None else x_
        zl_ = zl if zl_ is None else zl_
        core_ = core if core_ is None else core_
        return (y_ * 4 + zh_, (x_ * 4 + zl_) * 2 + core_)

    def along(axis, offset):
        if axis == "y":
            return device(y_=ring_add(offset, y))
        if axis == "zh":
            return device(zh_=ring_add(offset, zh))
        if axis == "x":
            return device(x_=ring_add(offset, x))
        if axis == "zl":
            return device(zl_=ring_add(offset, zl))
        return device(core_=other)

    copies = []

    def send(source, target, to):
        at = len(copies)
        copy = pltpu.make_async_remote_copy(
            src_ref=source, dst_ref=target,
            send_sem=send_sem.at[at], recv_sem=recv_sem.at[at],
            device_id=to, device_id_type=pl.DeviceIdType.MESH,
        )
        copies.append(copy)
        copy.start()
        return copy

    loads = []
    for at, (source, target) in reversed(list(enumerate(
        ((gate_hbm, gate_w), (up_hbm, up_w), (down_hbm, down_w), (tokens, token_in))
    ))):
        load = pltpu.make_async_copy(source, target, load_sem.at[at])
        load.start()
        loads.insert(0, load)

    def z_partner(offset):
        z = lax.rem(zh * 4 + zl + offset, 16)
        return device(zh_=lax.div(z, 4), zl_=lax.rem(z, 4))

    def plane_partner(offset):
        return device(x_=ring_add(offset // 4, x), y_=ring_add(offset % 4, y))

    groups = (
        [along("core", 1)],
        [z_partner(o) for o in range(1, 16)],
        [plane_partner(o) for o in range(1, 16)],
    )
    partners = [partner for group in groups for partner in group]
    barrier = pltpu.get_barrier_semaphore()
    for partner in partners:
        pl.semaphore_signal(barrier, inc=1, device_id=partner, device_id_type=pl.DeviceIdType.MESH)
    pl.semaphore_wait(barrier, len(partners))

    def peak_start(use, stage, tile):
        at = 3 * use + stage
        peak_send[at] = tile
        return [
            send(peak_send.at[at], peak_recv.at[at, o], to) for o, to in enumerate(groups[stage])
        ]

    def peak_end(use, stage, sent, tile):
        for o, copy in enumerate(sent):
            copy.wait_recv()
            tile = jnp.maximum(tile, peak_recv[3 * use + stage, o])
        return tile

    loads[3].wait()
    token_pad[0:12, :] = token_in[...].astype(F32)
    token_pad[12:16, :] = jnp.zeros((4, 768), F32)
    padded = token_pad[...]
    token_z[zl] = padded.astype(BF16)
    tile = fold_max(padded)
    peak_sent = peak_start(0, 0, tile)
    zl_sent = [send(token_z.at[zl], token_z.at[zl], along("zl", o)) for o in (1, 2, 3)]
    tile = peak_end(0, 0, peak_sent, tile)
    peak_sent = peak_start(0, 1, tile)
    for copy in zl_sent:
        copy.wait_recv()
    for i in range(4):
        token_f[12 * i : 12 * i + 12, :] = token_z[i].astype(F32)[0:12, :]
    token_x[x, core] = token_f[...].astype(BF16)
    mine = token_x.at[x, core]
    core_sent = [send(mine, mine, along("core", 1))]
    x_sent = [send(mine, mine, along("x", o)) for o in (1, 3, 2)]
    for o in (0, 1):
        x_sent[o].wait_recv()
        block = token_x.at[ring_add((3, 1)[o], x), core]
        core_sent.append(send(block, block, along("core", 1)))
    tile = peak_end(0, 1, peak_sent, tile)
    peak_sent = peak_start(0, 2, tile)
    x_sent[2].wait_recv()
    block = token_x.at[ring_add(2, x), core]
    core_sent.append(send(block, block, along("core", 1)))
    for copy in core_sent:
        copy.wait_recv()
    tile = peak_end(0, 2, peak_sent, tile)
    level, inverse = levels(tile, 1.0)
    for j in range(4):
        for c in range(2):
            values = token_x[ring_add(j, y), c].astype(F32)
            row = 96 * j + 48 * c
            scaled[row : row + 48, :] = (level * jnp.tanh(values * inverse)).astype(BF16)

    loads[0].wait()
    loads[1].wait()

    state = [dict() for _ in PIECES]

    def ring_first(axis, sends, receives):
        ends = (along(axis, 1), along(axis, 3))
        return [send(sends(m), receives(m), ends[m % 2]) for m in range(4)]

    def ring_second(axis, m, sends, receives):
        return send(sends(m), receives(m), along(axis, 1 if m == 4 else 3))

    def quarter(k, q):
        if PIECES[k][1] == 2:
            return lax.rem(q, 2), pl.multiple_of(lax.div(q, 2) * 48, 48), 48
        return 0, pl.multiple_of(q * 32, 32), 32

    def multiply(k):
        first, count = PIECES[k]
        columns = slice(128 * first, 128 * (first + count))
        gate = jnp.dot(scaled[...], gate_w[:, columns], preferred_element_type=F32)
        for t in range(count):
            lanes = slice(128 * t, 128 * t + 128)
            y_send[0, first + t] = gate[192:288, lanes].astype(BF16)
            y_send[3, first + t] = gate[288:384, lanes].astype(BF16)
            keep[0, first + t] = gate[0:96, lanes]
            keep[1, first + t] = gate[96:192, lanes]
        up = jnp.dot(scaled[...], up_w[:, columns], preferred_element_type=F32)
        for t in range(count):
            lanes = slice(128 * t, 128 * t + 128)
            y_send[1, first + t] = up[192:288, lanes].astype(BF16)
            y_send[2, first + t] = up[96:192, lanes].astype(BF16)
            keep[2, first + t] = up[0:96, lanes]
            keep[3, first + t] = up[288:384, lanes]
        state[k]["y"] = ring_first(
            "y",
            lambda m: y_send.at[m, pl.ds(first, count)],
            lambda m: y_recv.at[m, pl.ds(first, count)],
        )

    def y_second(k):
        first, count = PIECES[k]
        for m, source, own in ((4, 0, 1), (5, 1, 3)):
            state[k]["y"][source].wait_recv()
            for t in range(first, first + count):
                y_send[m, t] = (keep[own, t] + y_recv[source, t].astype(F32)).astype(BF16)
            state[k]["y"].append(
                ring_second(
                    "y", m,
                    lambda m: y_send.at[m, pl.ds(first, count)],
                    lambda m: y_recv.at[m, pl.ds(first, count)],
                )
            )

    def z_read(k, g, q):
        tile_at, row, rows = quarter(k, q)
        if PIECES[k][1] == 2:
            return z_sum[k, g, tile_at, pl.ds(row, rows), :]
        return z_sum1[g, pl.ds(row, rows), :]

    def z_rows(k):
        return quarter(k, 0)[2]

    def y_third(k):
        first, count = PIECES[k]
        for m in (2, 3, 4, 5):
            state[k]["y"][m].wait_recv()
        for t in range(count):
            for g, own, one, two in ((0, 0, 3, 4), (1, 2, 2, 5)):
                total = (
                    keep[own, first + t]
                    + y_recv[one, first + t].astype(F32)
                    + y_recv[two, first + t].astype(F32)
                )
                if count == 2:
                    z_sum[k, g, t] = total
                else:
                    z_sum1[g, 0:96, :] = total
        if count == 1:
            z_sum1[:, 96:128, :] = jnp.zeros((2, 32, 128), F32)
        rows = z_rows(k)
        state[k]["z"] = []
        for o in (2, 1, 3):
            for g in range(2):
                z_send[k, o - 1, g, 0:rows, :] = z_read(k, g, ring_add(o, zh)).astype(BF16)
            state[k]["z"].append(
                send(
                    z_send.at[k, o - 1, :, pl.ds(0, rows)],
                    z_recv.at[k, o - 1, :, pl.ds(0, rows)],
                    along("zh", o),
                )
            )

    def act_ref(k, owner_y, q):
        tile_at, row, rows = quarter(k, q)
        if PIECES[k][1] == 2:
            start = pl.multiple_of(owner_y * 96 + row, 16)
            return act.at[PIECES[k][0] + tile_at, pl.ds(start, rows), :]
        return act1.at[owner_y, pl.ds(row, rows), :]

    peaks = []

    def z_third(k):
        rows = z_rows(k)
        for copy in state[k]["z"]:
            copy.wait_recv()
        gate, up = (
            z_read(k, g, zh) + sum(z_recv[k, o, g, 0:rows, :].astype(F32) for o in range(3))
            for g in range(2)
        )
        value = gate / (1.0 + jnp.exp(-gate)) * up
        peaks.append(fold_max(value))
        mine = act_ref(k, y, zh)
        mine[...] = value.astype(BF16)
        state[k]["az"] = [send(mine, mine, along("zh", o)) for o in (2, 1, 3)]

    def act_z_end(k):
        for copy in state[k]["az"]:
            copy.wait_recv()
        first, count = PIECES[k]
        if count == 2:
            mine = act.at[pl.ds(first, 2), pl.ds(pl.multiple_of(y * 96, 96), 96), :]
        else:
            mine = act1.at[y, pl.ds(0, 96), :]
        state[k]["ay"] = [send(mine, mine, along("y", o)) for o in (2, 1, 3)]

    def act_y_end(k):
        for copy in state[k]["ay"]:
            copy.wait_recv()

    def every(step, count=len(PIECES)):
        for k in range(count):
            step(k)

    for step, k in (
        (multiply, 0), (multiply, 1), (y_second, 0), (multiply, 2), (y_second, 1),
        (multiply, 3), (y_third, 0), (y_second, 2), (y_third, 1), (y_second, 3),
        (y_third, 2), (y_third, 3),
    ):
        step(k)
    every(z_third)
    tile = peaks[0]
    for more in peaks[1:]:
        tile = jnp.maximum(tile, more)
    peak_sent = peak_start(1, 0, tile)
    act_z_end(0)
    tile = peak_end(1, 0, peak_sent, tile)
    peak_sent = peak_start(1, 1, tile)
    for k in range(1, len(PIECES)):
        act_z_end(k)
    tile = peak_end(1, 1, peak_sent, tile)
    peak_sent = peak_start(1, 2, tile)
    every(act_y_end)
    tile = peak_end(1, 2, peak_sent, tile)
    level, inverse = levels(tile, 0.125)

    def saturated(values):
        return (level * jnp.tanh(values.astype(F32) * inverse)).astype(BF16)

    for t in range(6):
        scaled_act[:, 128 * t : 128 * t + 128] = saturated(act[t])
    for d in range(4):
        scaled_act[96 * d : 96 * d + 96, 768:896] = saturated(act1[d, 0:96, :])

    loads[2].wait()

    downs = [dict() for _ in range(3)]

    def down_multiply(n):
        result = jnp.dot(
            scaled_act[...], down_w[:, 256 * n : 256 * n + 256], preferred_element_type=F32
        )
        for half in range(2):
            for d in range(4):
                for c in range(2):
                    row = 96 * d + 48 * c
                    down_part[n, half, c, d] = result[row : row + 48, 128 * half : 128 * half + 128]
        core_send[n] = down_part[n, :, other].astype(BF16)
        downs[n]["core"] = send(core_send.at[n], core_recv.at[n], along("core", 1))

    def down_read(n, half, j):
        d = ring_add(j, x)
        return down_part[n, half, core, d] + core_recv[n, half, d].astype(F32)

    def down_x_first(n):
        downs[n]["core"].wait_recv()
        downs[n]["x"] = []
        for o in (2, 1, 3):
            for half in range(2):
                x_send[n, o - 1, half] = down_read(n, half, o).astype(BF16)
            downs[n]["x"].append(send(x_send.at[n, o - 1], x_recv.at[n, o - 1], along("x", o)))

    def down_l_first(n):
        for copy in downs[n]["x"]:
            copy.wait_recv()
        for half in range(2):
            total = down_read(n, half, 0) + sum(x_recv[n, o, half].astype(F32) for o in range(3))
            for i in range(4):
                rows = total if i == 0 else pltpu.roll(total, 48 - 12 * i, 0)
                l_own[n, i, half] = rows[0:16, :]
                l_send[n, i, half] = rows[0:16, :].astype(BF16)
        downs[n]["l"] = [
            send(l_send.at[n, ring_add(o, zl)], l_recv.at[n, o], along("zl", o)) for o in (1, 2, 3)
        ]

    def down_last(n):
        for copy in downs[n]["l"]:
            copy.wait_recv()
        for half in range(2):
            total = l_own[n, zl, half]
            for o in (1, 2, 3):
                total = total + l_recv[n, o, half].astype(F32)
            lanes = slice(256 * n + 128 * half, 256 * n + 128 * half + 128)
            out[:, lanes] = (token_pad[0:12, lanes] + total[0:12, :]).astype(BF16)

    for step in (down_multiply, down_x_first, down_l_first, down_last):
        every(step, 3)

    for copy in copies:
        copy.wait_send()


def on_device(tokens, gate_weight, up_weight, down_weight):
    vmem = pltpu.VMEM
    return pl.pallas_call(
        kernel,
        out_shape=jax.ShapeDtypeStruct((12, 768), BF16),
        in_specs=[pl.BlockSpec(memory_space=pl.ANY)] * 4,
        out_specs=pl.BlockSpec(memory_space=pltpu.VMEM),
        scratch_shapes=[
            vmem((768, 896), BF16),
            vmem((768, 896), BF16),
            vmem((896, 768), BF16),
            vmem((12, 768), BF16),
            vmem((16, 768), F32),
            vmem((4, 16, 768), BF16),
            vmem((48, 768), F32),
            vmem((4, 2, 48, 768), BF16),
            vmem((384, 768), BF16),
            vmem((4, 7, 96, 128), F32),
            vmem((6, 7, 96, 128), BF16),
            vmem((6, 7, 96, 128), BF16),
            vmem((3, 2, 2, 96, 128), F32),
            vmem((2, 128, 128), F32),
            vmem((4, 3, 2, 48, 128), BF16),
            vmem((4, 3, 2, 48, 128), BF16),
            vmem((6, 384, 128), BF16),
            vmem((4, 128, 128), BF16),
            vmem((384, 896), BF16),
            vmem((3, 2, 2, 4, 48, 128), F32),
            vmem((3, 2, 4, 48, 128), BF16),
            vmem((3, 2, 4, 48, 128), BF16),
            vmem((3, 3, 2, 48, 128), BF16),
            vmem((3, 3, 2, 48, 128), BF16),
            vmem((3, 4, 2, 16, 128), F32),
            vmem((3, 4, 2, 16, 128), BF16),
            vmem((3, 4, 2, 16, 128), BF16),
            vmem((6, 8, 128), F32),
            vmem((6, 15, 8, 128), F32),
            pltpu.SemaphoreType.DMA((MAX_COPIES,)),
            pltpu.SemaphoreType.DMA((MAX_COPIES,)),
            pltpu.SemaphoreType.DMA((4,)),
        ],
        compiler_params=pltpu.CompilerParams(
            collective_id=0, has_side_effects=True, vmem_limit_bytes=60 * 1024 * 1024
        ),
        cost_estimate=pl.CostEstimate(
            flops=6 * 384 * 768 * 896, bytes_accessed=3 * 2 * 768 * 896, transcendentals=1000000
        ),
        name="swiglu_block",
    )(tokens, gate_weight, up_weight, down_weight)


def solution(mesh):
    in_specs = (
        P("hidden", "width"),
        P("width", "hidden"),
        P("width", "hidden"),
        P("hidden", "width"),
    )
    return jax.shard_map(
        on_device, mesh=mesh, in_specs=in_specs, out_specs=P("hidden", "width"), check_vma=False
    )
```

```python
import jax
import jax.numpy as jnp
from jax import lax
from jax.experimental import pallas as pl
from jax.experimental.pallas import tpu as pltpu
from jax.sharding import PartitionSpec as P

F32 = jnp.float32
BF16 = jnp.bfloat16

PIECES = ((6, 1), (0, 2), (2, 2), (4, 2))
Y_RING = (False, True, True, True)
Z_RING = (False, True, True, False)
STEPS = [(name[0], int(name[1])) for name in (
    "M0", "M1", "M2", "M3", "N1", "N2", "S1", "S2", "N3", "Y0",
    "S3", "Y1", "Y2", "Y3", "A0", "Z1", "Z2", "A3", "A1", "A2",
)]
Z_ORDER = sorted(range(1, 16), key=lambda o: -min(o, 16 - o))
PLANE_ORDER = sorted(range(1, 16), key=lambda o: abs(o // 4 - 2) + abs(o % 4 - 2))
MAX_COPIES = 256


def ring_add(offset, value):
    return lax.rem(value + offset, 4)


def fold_max(values):
    rows, columns = values.shape
    total = None
    for row in range(0, rows, 8):
        for column in range(0, columns, 128):
            tile = jnp.abs(values[row : row + 8, column : column + 128])
            total = tile if total is None else jnp.maximum(total, tile)
    return jnp.max(total, axis=0, keepdims=True)


def levels(tile, factor):
    peak = jnp.max(tile, axis=1, keepdims=True)
    level = 0.5 * (factor * peak + 1e-06)
    return level, 1.0 / level


def kernel(
    tokens, gate_hbm, up_hbm, down_hbm, out,
    gate_w, up_w, down_w, token_in, token_pad, token_z, token_f, token_x, scaled,
    keep, y_send, y_recv, z_sum, z_sum1, z_send, z_recv, act, act1, scaled_act,
    down_part, core_send, core_recv, x_send, x_recv, l_own, l_send, l_recv,
    peak_send, peak_recv, send_sem, recv_sem, load_sem,
):
    width, hidden = lax.axis_index("width"), lax.axis_index("hidden")
    y, zh = lax.div(width, 4), lax.rem(width, 4)
    core = lax.rem(hidden, 2)
    x, zl = lax.div(hidden, 8), lax.rem(lax.div(hidden, 2), 4)
    other = 1 - core

    def device(y_=None, zh_=None, x_=None, zl_=None, core_=None):
        y_ = y if y_ is None else y_
        zh_ = zh if zh_ is None else zh_
        x_ = x if x_ is None else x_
        zl_ = zl if zl_ is None else zl_
        core_ = core if core_ is None else core_
        return (y_ * 4 + zh_, (x_ * 4 + zl_) * 2 + core_)

    def along(axis, offset):
        if axis == "y":
            return device(y_=ring_add(offset, y))
        if axis == "zh":
            return device(zh_=ring_add(offset, zh))
        if axis == "x":
            return device(x_=ring_add(offset, x))
        if axis == "zl":
            return device(zl_=ring_add(offset, zl))
        return device(core_=other)

    copies = []

    def send(source, target, to):
        at = len(copies)
        copy = pltpu.make_async_remote_copy(
            src_ref=source, dst_ref=target,
            send_sem=send_sem.at[at], recv_sem=recv_sem.at[at],
            device_id=to, device_id_type=pl.DeviceIdType.MESH,
        )
        copies.append(copy)
        copy.start()
        return copy

    loads = []
    for at, (source, target) in reversed(list(enumerate(
        ((gate_hbm, gate_w), (up_hbm, up_w), (down_hbm, down_w), (tokens, token_in))
    ))):
        load = pltpu.make_async_copy(source, target, load_sem.at[at])
        load.start()
        loads.insert(0, load)

    def z_partner(offset):
        z = lax.rem(zh * 4 + zl + offset, 16)
        return device(zh_=lax.div(z, 4), zl_=lax.rem(z, 4))

    def plane_partner(offset):
        return device(x_=ring_add(offset // 4, x), y_=ring_add(offset % 4, y))

    groups = (
        [along("core", 1)],
        [z_partner(o) for o in Z_ORDER],
        [plane_partner(o) for o in PLANE_ORDER],
    )
    partners = groups[1] + groups[2] + groups[0]
    barrier = pltpu.get_barrier_semaphore()
    for partner in partners:
        pl.semaphore_signal(barrier, inc=1, device_id=partner, device_id_type=pl.DeviceIdType.MESH)
    pl.semaphore_wait(barrier, len(partners))

    def peak_start(use, stage, tile):
        at = 3 * use + stage
        peak_send[at] = tile
        return [
            send(peak_send.at[at], peak_recv.at[at, o], to) for o, to in enumerate(groups[stage])
        ]

    def peak_end(use, stage, sent, tile):
        for o, copy in enumerate(sent):
            copy.wait_recv()
            tile = jnp.maximum(tile, peak_recv[3 * use + stage, o])
        return tile

    loads[3].wait()
    token_pad[0:12, :] = token_in[...].astype(F32)
    token_pad[12:16, :] = jnp.zeros((4, 768), F32)
    padded = token_pad[...]
    token_z[zl] = padded.astype(BF16)
    tile = fold_max(padded)
    peak_sent = peak_start(0, 0, tile)
    zl_sent = [send(token_z.at[zl], token_z.at[zl], along("zl", o)) for o in (1, 2, 3)]
    tile = peak_end(0, 0, peak_sent, tile)
    peak_sent = peak_start(0, 1, tile)
    for copy in zl_sent:
        copy.wait_recv()
    for i in range(4):
        token_f[12 * i : 12 * i + 12, :] = token_z[i].astype(F32)[0:12, :]
    token_x[x, core] = token_f[...].astype(BF16)
    mine = token_x.at[x, core]
    core_sent = [send(mine, mine, along("core", 1))]
    x_sent = [send(mine, mine, along("x", o)) for o in (1, 3, 2)]
    for o in (0, 1):
        x_sent[o].wait_recv()
        block = token_x.at[ring_add((3, 1)[o], x), core]
        core_sent.append(send(block, block, along("core", 1)))
    tile = peak_end(0, 1, peak_sent, tile)
    peak_sent = peak_start(0, 2, tile)
    x_sent[2].wait_recv()
    block = token_x.at[ring_add(2, x), core]
    core_sent.append(send(block, block, along("core", 1)))
    for copy in core_sent:
        copy.wait_recv()
    tile = peak_end(0, 2, peak_sent, tile)
    level, inverse = levels(tile, 1.0)
    for j in range(4):
        for c in range(2):
            values = token_x[ring_add(j, y), c].astype(F32)
            row = 96 * j + 48 * c
            scaled[row : row + 48, :] = (level * jnp.tanh(values * inverse)).astype(BF16)

    loads[0].wait()
    loads[1].wait()

    state = [dict() for _ in PIECES]

    def ring_sends(axis, which, sends, receives):
        ends = (along(axis, 1), along(axis, 3))
        return {m: send(sends(m), receives(m), ends[m % 2]) for m in which}

    def quarter(k, q):
        if PIECES[k][1] == 2:
            return lax.rem(q, 2), pl.multiple_of(lax.div(q, 2) * 48, 48), 48
        return 0, pl.multiple_of(q * 32, 32), 32

    def y_ring(k, which):
        tiles = pl.ds(*PIECES[k])
        return ring_sends("y", which, lambda m: y_send.at[m, tiles], lambda m: y_recv.at[m, tiles])

    def y_near(k):
        state[k]["y"].update(y_ring(k, (2, 3)))

    def z_ring(k, which):
        return ring_sends("zh", which, lambda m: z_slot(z_send, k, m), lambda m: z_slot(z_recv, k, m))

    def multiply(k):
        first, count = PIECES[k]
        columns = slice(128 * first, 128 * (first + count))
        gate = jnp.dot(scaled[...], gate_w[:, columns], preferred_element_type=F32)
        up = jnp.dot(scaled[...], up_w[:, columns], preferred_element_type=F32)
        tiles = pl.ds(first, count)
        for t in range(count):
            lanes = slice(128 * t, 128 * t + 128)
            if Y_RING[k]:
                y_send[0, first + t] = gate[192:288, lanes].astype(BF16)
                y_send[1, first + t] = up[192:288, lanes].astype(BF16)
                y_send[2, first + t] = up[96:192, lanes].astype(BF16)
                y_send[3, first + t] = gate[288:384, lanes].astype(BF16)
                keep[1, first + t] = gate[96:192, lanes]
                keep[3, first + t] = up[288:384, lanes]
            else:
                for o in range(3):
                    rows = slice(96 * o + 96, 96 * o + 192)
                    y_send[2 * o, first + t] = gate[rows, lanes].astype(BF16)
                    y_send[2 * o + 1, first + t] = up[rows, lanes].astype(BF16)
            keep[0, first + t] = gate[0:96, lanes]
            keep[2, first + t] = up[0:96, lanes]
        if Y_RING[k]:
            state[k]["y"] = y_ring(k, (0, 1))
        else:
            state[k]["y"] = [
                send(
                    y_send.at[pl.ds(2 * o - 2, 2), tiles],
                    y_recv.at[pl.ds(2 * o - 2, 2), tiles],
                    along("y", o),
                )
                for o in (2, 1, 3)
            ]

    def y_second(k):
        first, count = PIECES[k]
        for m, source, own in ((4, 0, 1), (5, 1, 3)):
            state[k]["y"][source].wait_recv()
            for t in range(first, first + count):
                y_send[m, t] = (keep[own, t] + y_recv[source, t].astype(F32)).astype(BF16)
            state[k]["y"].update(y_ring(k, (m,)))

    def z_read(k, g, q):
        tile_at, row, rows = quarter(k, q)
        if PIECES[k][1] == 2:
            return z_sum[PIECES[k][0] // 2, g, tile_at, pl.ds(row, rows), :]
        return z_sum1[g, pl.ds(row, rows), :]

    def z_rows(k):
        return quarter(k, 0)[2]

    def y_third(k):
        first, count = PIECES[k]
        ring = Y_RING[k]
        for m in (2, 3, 4, 5) if ring else range(3):
            state[k]["y"][m].wait_recv()
        for t in range(count):
            for g, arrived in ((0, (3, 4) if ring else (0, 2, 4)), (1, (2, 5) if ring else (1, 3, 5))):
                total = keep[2 * g, first + t]
                for m in arrived:
                    total = total + y_recv[m, first + t].astype(F32)
                if count == 2:
                    z_sum[PIECES[k][0] // 2, g, t] = total
                else:
                    z_sum1[g, 0:96, :] = total
        if count == 1:
            z_sum1[:, 96:128, :] = jnp.zeros((2, 32, 128), F32)
        rows = z_rows(k)
        if Z_RING[k]:
            for m, g, j in ((0, 0, 2), (1, 1, 2), (2, 1, 1), (3, 0, 3)):
                z_send[k, m // 2, m % 2, 0:rows, :] = z_read(k, g, ring_add(j, zh)).astype(BF16)
            state[k]["z"] = z_ring(k, range(4))
            return
        state[k]["z"] = []
        for o in (2, 1, 3):
            for g in range(2):
                z_send[k, o - 1, g, 0:rows, :] = z_read(k, g, ring_add(o, zh)).astype(BF16)
            state[k]["z"].append(
                send(
                    z_send.at[k, o - 1, :, pl.ds(0, rows)],
                    z_recv.at[k, o - 1, :, pl.ds(0, rows)],
                    along("zh", o),
                )
            )

    def z_slot(ref, k, m):
        return ref.at[k, m // 2, m % 2, pl.ds(0, z_rows(k))]

    def z_second(k):
        rows = z_rows(k)
        for m, g, j in ((4, 0, 1), (5, 1, 3)):
            state[k]["z"][m - 4].wait_recv()
            total = z_read(k, g, ring_add(j, zh)) + z_recv[k, 0, m - 4, 0:rows, :].astype(F32)
            z_send[k, 2, m - 4, 0:rows, :] = total.astype(BF16)
            state[k]["z"].update(z_ring(k, (m,)))

    def act_ref(k, owner_y, q):
        tile_at, row, rows = quarter(k, q)
        if PIECES[k][1] == 2:
            start = pl.multiple_of(owner_y * 96 + row, 16)
            return act.at[PIECES[k][0] + tile_at, pl.ds(start, rows), :]
        return act1.at[owner_y, pl.ds(row, rows), :]

    peaks = []

    def z_third(k):
        rows = z_rows(k)
        ring = Z_RING[k]
        for m in (2, 3, 4, 5) if ring else range(3):
            state[k]["z"][m].wait_recv()

        def summed(g, arrived):
            total = z_read(k, g, zh)
            for m in arrived:
                total = total + z_recv[k, m // 2, m % 2, 0:rows, :].astype(F32)
            return total

        gate = summed(0, (3, 4) if ring else (0, 2, 4))
        up = summed(1, (2, 5) if ring else (1, 3, 5))
        value = gate / (1.0 + jnp.exp(-gate)) * up
        peaks.append(fold_max(value))
        mine = act_ref(k, y, zh)
        mine[...] = value.astype(BF16)
        state[k]["az"] = [send(mine, mine, along("zh", o)) for o in (2, 1, 3)]

    def act_z_end(k):
        for copy in state[k]["az"]:
            copy.wait_recv()
        first, count = PIECES[k]
        if count == 2:
            mine = act.at[pl.ds(first, 2), pl.ds(pl.multiple_of(y * 96, 96), 96), :]
        else:
            mine = act1.at[y, pl.ds(0, 96), :]
        state[k]["ay"] = [send(mine, mine, along("y", o)) for o in (2, 1, 3)]

    def act_y_end(k):
        for copy in state[k]["ay"]:
            copy.wait_recv()

    def every(step, count=len(PIECES)):
        for k in range(count):
            step(k)

    for step, k in STEPS:
        {"M": multiply, "N": y_near, "S": y_second, "Y": y_third, "Z": z_second, "A": z_third}[step](k)
    tile = peaks[0]
    for more in peaks[1:]:
        tile = jnp.maximum(tile, more)
    peak_sent = peak_start(1, 0, tile)
    ended = [k for step, k in STEPS if step == "A"]
    act_z_end(ended[0])
    tile = peak_end(1, 0, peak_sent, tile)
    peak_sent = peak_start(1, 2, tile)
    for k in ended[1:]:
        act_z_end(k)
    tile = peak_end(1, 2, peak_sent, tile)
    peak_sent = peak_start(1, 1, tile)
    every(act_y_end)
    tile = peak_end(1, 1, peak_sent, tile)
    level, inverse = levels(tile, 0.125)

    def saturated(values):
        return (level * jnp.tanh(values.astype(F32) * inverse)).astype(BF16)

    for t in range(6):
        scaled_act[:, 128 * t : 128 * t + 128] = saturated(act[t])
    for d in range(4):
        scaled_act[96 * d : 96 * d + 96, 768:896] = saturated(act1[d, 0:96, :])

    loads[2].wait()

    downs = [dict() for _ in range(3)]

    def down_multiply(n):
        result = jnp.dot(
            scaled_act[...], down_w[:, 256 * n : 256 * n + 256], preferred_element_type=F32
        )
        for half in range(2):
            for d in range(4):
                for c in range(2):
                    row = 96 * d + 48 * c
                    down_part[n, half, c, d] = result[row : row + 48, 128 * half : 128 * half + 128]
        core_send[n] = down_part[n, :, other].astype(BF16)
        downs[n]["core"] = send(core_send.at[n], core_recv.at[n], along("core", 1))

    def down_read(n, half, j):
        d = ring_add(j, x)
        return down_part[n, half, core, d] + core_recv[n, half, d].astype(F32)

    def down_x_first(n):
        downs[n]["core"].wait_recv()
        downs[n]["x"] = []
        for o in (2, 1, 3):
            for half in range(2):
                x_send[n, o - 1, half] = down_read(n, half, o).astype(BF16)
            downs[n]["x"].append(send(x_send.at[n, o - 1], x_recv.at[n, o - 1], along("x", o)))

    def down_l_first(n):
        for copy in downs[n]["x"]:
            copy.wait_recv()
        for half in range(2):
            total = down_read(n, half, 0) + sum(x_recv[n, o, half].astype(F32) for o in range(3))
            for i in range(4):
                rows = total if i == 0 else pltpu.roll(total, 48 - 12 * i, 0)
                l_own[n, i, half] = rows[0:16, :]
                l_send[n, i, half] = rows[0:16, :].astype(BF16)
        downs[n]["l"] = [
            send(l_send.at[n, ring_add(o, zl)], l_recv.at[n, o], along("zl", o)) for o in (1, 2, 3)
        ]

    def down_last(n):
        for copy in downs[n]["l"]:
            copy.wait_recv()
        for half in range(2):
            total = l_own[n, zl, half]
            for o in (1, 2, 3):
                total = total + l_recv[n, o, half].astype(F32)
            lanes = slice(256 * n + 128 * half, 256 * n + 128 * half + 128)
            out[:, lanes] = (token_pad[0:12, lanes] + total[0:12, :]).astype(BF16)

    for step, n in (
        (down_multiply, 0), (down_multiply, 1), (down_x_first, 0), (down_multiply, 2),
        (down_x_first, 1), (down_x_first, 2), (down_l_first, 0), (down_l_first, 1),
        (down_l_first, 2), (down_last, 0), (down_last, 1), (down_last, 2),
    ):
        step(n)

    for copy in copies:
        copy.wait_send()


def on_device(tokens, gate_weight, up_weight, down_weight):
    vmem = pltpu.VMEM
    return pl.pallas_call(
        kernel,
        out_shape=jax.ShapeDtypeStruct((12, 768), BF16),
        in_specs=[pl.BlockSpec(memory_space=pl.ANY)] * 4,
        out_specs=pl.BlockSpec(memory_space=pltpu.VMEM),
        scratch_shapes=[
            vmem((768, 896), BF16),
            vmem((768, 896), BF16),
            vmem((896, 768), BF16),
            vmem((12, 768), BF16),
            vmem((16, 768), F32),
            vmem((4, 16, 768), BF16),
            vmem((48, 768), F32),
            vmem((4, 2, 48, 768), BF16),
            vmem((384, 768), BF16),
            vmem((4, 7, 96, 128), F32),
            vmem((6, 7, 96, 128), BF16),
            vmem((6, 7, 96, 128), BF16),
            vmem((3, 2, 2, 96, 128), F32),
            vmem((2, 128, 128), F32),
            vmem((4, 3, 2, 48, 128), BF16),
            vmem((4, 3, 2, 48, 128), BF16),
            vmem((6, 384, 128), BF16),
            vmem((4, 128, 128), BF16),
            vmem((384, 896), BF16),
            vmem((3, 2, 2, 4, 48, 128), F32),
            vmem((3, 2, 4, 48, 128), BF16),
            vmem((3, 2, 4, 48, 128), BF16),
            vmem((3, 3, 2, 48, 128), BF16),
            vmem((3, 3, 2, 48, 128), BF16),
            vmem((3, 4, 2, 16, 128), F32),
            vmem((3, 4, 2, 16, 128), BF16),
            vmem((3, 4, 2, 16, 128), BF16),
            vmem((6, 1, 128), F32),
            vmem((6, 15, 1, 128), F32),
            pltpu.SemaphoreType.DMA((MAX_COPIES,)),
            pltpu.SemaphoreType.DMA((MAX_COPIES,)),
            pltpu.SemaphoreType.DMA((4,)),
        ],
        compiler_params=pltpu.CompilerParams(
            collective_id=0, has_side_effects=True, vmem_limit_bytes=60 * 1024 * 1024
        ),
        cost_estimate=pl.CostEstimate(
            flops=6 * 384 * 768 * 896, bytes_accessed=3 * 2 * 768 * 896, transcendentals=1000000
        ),
        name="swiglu_block",
    )(tokens, gate_weight, up_weight, down_weight)


def solution(mesh):
    in_specs = (
        P("hidden", "width"),
        P("width", "hidden"),
        P("width", "hidden"),
        P("hidden", "width"),
    )
    return jax.shard_map(
        on_device, mesh=mesh, in_specs=in_specs, out_specs=P("hidden", "width"), check_vma=False
    )
```

```python
import jax
import jax.numpy as jnp
from jax import lax
from jax.experimental import pallas as pl
from jax.experimental.pallas import tpu as pltpu
from jax.sharding import PartitionSpec as P

F32 = jnp.float32
BF16 = jnp.bfloat16

PIECES = ((6, 1), (0, 2), (2, 2), (4, 2))
Y_RING = (False, True, True, True)
Z_RING = (False, True, True, True)
STEPS = [(name[0], int(name[1])) for name in (
    "M0", "M1", "M2", "M3", "N1", "N2", "S1", "S2", "N3", "Y0",
    "S3", "Y1", "Y2", "P1", "Y3", "P2", "P3", "A0", "Z1", "Z2",
    "Z3", "A1", "A2", "A3",
)]
Z_ORDER = sorted(range(1, 16), key=lambda o: -min(o, 16 - o))
PLANE_ORDER = sorted(range(1, 16), key=lambda o: abs(o // 4 - 2) + abs(o % 4 - 2))
MAX_COPIES = 256


def ring_add(offset, value):
    return lax.rem(value + offset, 4)


def fold_max(values):
    rows, columns = values.shape
    total = None
    for row in range(0, rows, 8):
        for column in range(0, columns, 128):
            tile = jnp.abs(values[row : row + 8, column : column + 128])
            total = tile if total is None else jnp.maximum(total, tile)
    return jnp.max(total, axis=0, keepdims=True)


def levels(tile, factor):
    peak = jnp.max(tile, axis=1, keepdims=True)
    level = 0.5 * (factor * peak + 1e-06)
    return level, 1.0 / level


def kernel(
    tokens, gate_hbm, up_hbm, down_hbm, out,
    gate_w, up_w, down_w, token_in, token_pad, token_z, token_f, token_x, scaled,
    keep, y_send, y_recv, z_sum, z_sum1, z_send, z_recv, act, act1, scaled_act,
    down_total, down_part, core_send, core_recv, x_send, x_recv, l_own, l_send, l_recv,
    peak_send, peak_recv, send_sem, recv_sem, load_sem,
):
    width, hidden = lax.axis_index("width"), lax.axis_index("hidden")
    y, zh = lax.div(width, 4), lax.rem(width, 4)
    core = lax.rem(hidden, 2)
    x, zl = lax.div(hidden, 8), lax.rem(lax.div(hidden, 2), 4)
    other = 1 - core

    def device(y_=None, zh_=None, x_=None, zl_=None, core_=None):
        y_ = y if y_ is None else y_
        zh_ = zh if zh_ is None else zh_
        x_ = x if x_ is None else x_
        zl_ = zl if zl_ is None else zl_
        core_ = core if core_ is None else core_
        return (y_ * 4 + zh_, (x_ * 4 + zl_) * 2 + core_)

    def along(axis, offset):
        if axis == "y":
            return device(y_=ring_add(offset, y))
        if axis == "zh":
            return device(zh_=ring_add(offset, zh))
        if axis == "x":
            return device(x_=ring_add(offset, x))
        if axis == "zl":
            return device(zl_=ring_add(offset, zl))
        return device(core_=other)

    copies = []

    def send(source, target, to):
        at = len(copies)
        copy = pltpu.make_async_remote_copy(
            src_ref=source, dst_ref=target,
            send_sem=send_sem.at[at], recv_sem=recv_sem.at[at],
            device_id=to, device_id_type=pl.DeviceIdType.MESH,
        )
        copies.append(copy)
        copy.start()
        return copy

    loads = []
    for at, (source, target) in reversed(list(enumerate(
        ((gate_hbm, gate_w), (up_hbm, up_w), (down_hbm, down_w), (tokens, token_in))
    ))):
        load = pltpu.make_async_copy(source, target, load_sem.at[at])
        load.start()
        loads.insert(0, load)

    def z_partner(offset):
        z = lax.rem(zh * 4 + zl + offset, 16)
        return device(zh_=lax.div(z, 4), zl_=lax.rem(z, 4))

    def plane_partner(offset):
        return device(x_=ring_add(offset // 4, x), y_=ring_add(offset % 4, y))

    groups = (
        [along("core", 1)],
        [z_partner(o) for o in Z_ORDER],
        [plane_partner(o) for o in PLANE_ORDER],
    )
    partners = groups[1] + groups[2] + groups[0]
    barrier = pltpu.get_barrier_semaphore()
    for partner in partners:
        pl.semaphore_signal(barrier, inc=1, device_id=partner, device_id_type=pl.DeviceIdType.MESH)
    pl.semaphore_wait(barrier, len(partners))

    def peak_start(use, stage, tile):
        at = 3 * use + stage
        peak_send[at] = tile
        return [
            send(peak_send.at[at], peak_recv.at[at, o], to) for o, to in enumerate(groups[stage])
        ]

    def peak_end(use, stage, sent, tile):
        for o, copy in enumerate(sent):
            copy.wait_recv()
            tile = jnp.maximum(tile, peak_recv[3 * use + stage, o])
        return tile

    loads[3].wait()
    token_pad[0:12, :] = token_in[...].astype(F32)
    token_pad[12:16, :] = jnp.zeros((4, 768), F32)
    padded = token_pad[...]
    token_z[zl] = padded.astype(BF16)
    tile = fold_max(padded)
    peak_sent = peak_start(0, 0, tile)
    zl_sent = [send(token_z.at[zl], token_z.at[zl], along("zl", o)) for o in (1, 2, 3)]
    tile = peak_end(0, 0, peak_sent, tile)
    peak_sent = peak_start(0, 1, tile)
    for copy in zl_sent:
        copy.wait_recv()
    for i in range(4):
        token_f[12 * i : 12 * i + 12, :] = token_z[i].astype(F32)[0:12, :]
    token_x[x, core] = token_f[...].astype(BF16)
    mine = token_x.at[x, core]
    core_sent = [send(mine, mine, along("core", 1))]
    x_sent = [send(mine, mine, along("x", o)) for o in (1, 3, 2)]
    for o in (0, 1):
        x_sent[o].wait_recv()
        block = token_x.at[ring_add((3, 1)[o], x), core]
        core_sent.append(send(block, block, along("core", 1)))
    tile = peak_end(0, 1, peak_sent, tile)
    peak_sent = peak_start(0, 2, tile)
    x_sent[2].wait_recv()
    block = token_x.at[ring_add(2, x), core]
    core_sent.append(send(block, block, along("core", 1)))
    for copy in core_sent:
        copy.wait_recv()
    tile = peak_end(0, 2, peak_sent, tile)
    level, inverse = levels(tile, 1.0)
    for j in range(4):
        for c in range(2):
            values = token_x[ring_add(j, y), c].astype(F32)
            row = 96 * j + 48 * c
            scaled[row : row + 48, :] = (level * jnp.tanh(values * inverse)).astype(BF16)

    loads[0].wait()
    loads[1].wait()

    state = [dict() for _ in PIECES]

    def ring_sends(axis, which, sends, receives):
        ends = (along(axis, 1), along(axis, 3))
        return {m: send(sends(m), receives(m), ends[m % 2]) for m in which}

    def quarter(k, q):
        if PIECES[k][1] == 2:
            return lax.rem(q, 2), pl.multiple_of(lax.div(q, 2) * 48, 48), 48
        return 0, pl.multiple_of(q * 32, 32), 32

    def y_ring(k, which):
        tiles = pl.ds(*PIECES[k])
        return ring_sends("y", which, lambda m: y_send.at[m, tiles], lambda m: y_recv.at[m, tiles])

    def y_near(k):
        state[k]["y"].update(y_ring(k, (2, 3)))

    def z_ring(k, which):
        return ring_sends("zh", which, lambda m: z_slot(z_send, k, m), lambda m: z_slot(z_recv, k, m))

    def multiply(k):
        first, count = PIECES[k]
        columns = slice(128 * first, 128 * (first + count))
        gate = jnp.dot(scaled[...], gate_w[:, columns], preferred_element_type=F32)
        up = jnp.dot(scaled[...], up_w[:, columns], preferred_element_type=F32)
        tiles = pl.ds(first, count)
        for t in range(count):
            lanes = slice(128 * t, 128 * t + 128)
            if Y_RING[k]:
                y_send[0, first + t] = gate[192:288, lanes].astype(BF16)
                y_send[1, first + t] = up[192:288, lanes].astype(BF16)
                y_send[2, first + t] = up[96:192, lanes].astype(BF16)
                y_send[3, first + t] = gate[288:384, lanes].astype(BF16)
                keep[1, first + t] = gate[96:192, lanes]
                keep[3, first + t] = up[288:384, lanes]
            else:
                for o in range(3):
                    rows = slice(96 * o + 96, 96 * o + 192)
                    y_send[2 * o, first + t] = gate[rows, lanes].astype(BF16)
                    y_send[2 * o + 1, first + t] = up[rows, lanes].astype(BF16)
            keep[0, first + t] = gate[0:96, lanes]
            keep[2, first + t] = up[0:96, lanes]
        if Y_RING[k]:
            state[k]["y"] = y_ring(k, (0, 1))
        else:
            state[k]["y"] = [
                send(
                    y_send.at[pl.ds(2 * o - 2, 2), tiles],
                    y_recv.at[pl.ds(2 * o - 2, 2), tiles],
                    along("y", o),
                )
                for o in (2, 1, 3)
            ]

    def y_second(k):
        first, count = PIECES[k]
        for m, source, own in ((4, 0, 1), (5, 1, 3)):
            state[k]["y"][source].wait_recv()
            for t in range(first, first + count):
                y_send[m, t] = (keep[own, t] + y_recv[source, t].astype(F32)).astype(BF16)
            state[k]["y"].update(y_ring(k, (m,)))

    def z_read(k, g, q):
        tile_at, row, rows = quarter(k, q)
        if PIECES[k][1] == 2:
            return z_sum[PIECES[k][0] // 2, g, tile_at, pl.ds(row, rows), :]
        return z_sum1[g, pl.ds(row, rows), :]

    def z_rows(k):
        return quarter(k, 0)[2]

    def y_third(k):
        first, count = PIECES[k]
        ring = Y_RING[k]
        for m in (2, 3, 4, 5) if ring else range(3):
            state[k]["y"][m].wait_recv()
        for t in range(count):
            for g, arrived in ((0, (3, 4) if ring else (0, 2, 4)), (1, (2, 5) if ring else (1, 3, 5))):
                total = keep[2 * g, first + t]
                for m in arrived:
                    total = total + y_recv[m, first + t].astype(F32)
                if count == 2:
                    z_sum[PIECES[k][0] // 2, g, t] = total
                else:
                    z_sum1[g, 0:96, :] = total
        if count == 1:
            z_sum1[:, 96:128, :] = jnp.zeros((2, 32, 128), F32)
        rows = z_rows(k)
        if Z_RING[k]:
            for m in range(2):
                z_send[k, 0, m, 0:rows, :] = z_read(k, m, ring_add(2, zh)).astype(BF16)
            state[k]["z"] = z_ring(k, (0, 1))
            return
        state[k]["z"] = []
        for o in (2, 1, 3):
            for g in range(2):
                z_send[k, o - 1, g, 0:rows, :] = z_read(k, g, ring_add(o, zh)).astype(BF16)
            state[k]["z"].append(
                send(
                    z_send.at[k, o - 1, :, pl.ds(0, rows)],
                    z_recv.at[k, o - 1, :, pl.ds(0, rows)],
                    along("zh", o),
                )
            )

    def z_near(k):
        rows = z_rows(k)
        z_send[k, 1, 0, 0:rows, :] = z_read(k, 1, ring_add(1, zh)).astype(BF16)
        z_send[k, 1, 1, 0:rows, :] = z_read(k, 0, ring_add(3, zh)).astype(BF16)
        state[k]["z"].update(z_ring(k, (2, 3)))

    def z_slot(ref, k, m):
        return ref.at[k, m // 2, m % 2, pl.ds(0, z_rows(k))]

    def z_second(k):
        rows = z_rows(k)
        for m, g, j in ((4, 0, 1), (5, 1, 3)):
            state[k]["z"][m - 4].wait_recv()
            total = z_read(k, g, ring_add(j, zh)) + z_recv[k, 0, m - 4, 0:rows, :].astype(F32)
            z_send[k, 2, m - 4, 0:rows, :] = total.astype(BF16)
            state[k]["z"].update(z_ring(k, (m,)))

    def act_ref(k, owner_y, q):
        tile_at, row, rows = quarter(k, q)
        if PIECES[k][1] == 2:
            start = pl.multiple_of(owner_y * 96 + row, 16)
            return act.at[PIECES[k][0] + tile_at, pl.ds(start, rows), :]
        return act1.at[owner_y, pl.ds(row, rows), :]

    peaks = []

    def z_third(k):
        rows = z_rows(k)
        ring = Z_RING[k]
        for m in (2, 3, 4, 5) if ring else range(3):
            state[k]["z"][m].wait_recv()

        def summed(g, arrived):
            total = z_read(k, g, zh)
            for m in arrived:
                total = total + z_recv[k, m // 2, m % 2, 0:rows, :].astype(F32)
            return total

        gate = summed(0, (3, 4) if ring else (0, 2, 4))
        up = summed(1, (2, 5) if ring else (1, 3, 5))
        value = gate / (1.0 + jnp.exp(-gate)) * up
        peaks.append(fold_max(value))
        mine = act_ref(k, y, zh)
        mine[...] = value.astype(BF16)
        state[k]["az"] = {o: send(mine, mine, along("zh", o)) for o in (2, 1, 3)}
        state[k]["ay"] = []
        pass_on(k, 0)

    def pass_on(k, o):
        block = act_ref(k, y, ring_add(4 - o, zh))
        state[k]["ay"] += [send(block, block, along("y", place)) for place in (2, 1, 3)]

    def act_near(k):
        for o in (1, 3):
            state[k]["az"][o].wait_recv()
            pass_on(k, o)

    def act_far(k):
        state[k]["az"][2].wait_recv()
        pass_on(k, 2)

    def act_y_end(k):
        for copy in state[k]["ay"]:
            copy.wait_recv()

    def every(step, count=len(PIECES)):
        for k in range(count):
            step(k)

    for step, k in STEPS:
        {"M": multiply, "N": y_near, "P": z_near, "S": y_second, "Y": y_third, "Z": z_second, "A": z_third}[step](k)
    tile = peaks[0]
    for more in peaks[1:]:
        tile = jnp.maximum(tile, more)
    peak_sent = peak_start(1, 0, tile)
    ended = [k for step, k in STEPS if step == "A"]
    act_near(ended[0])
    tile = peak_end(1, 0, peak_sent, tile)
    peak_sent = peak_start(1, 1, tile)
    for k in ended[1:]:
        act_near(k)
    for k in ended[:-1]:
        act_far(k)
    tile = peak_end(1, 1, peak_sent, tile)
    peak_sent = peak_start(1, 2, tile)
    act_far(ended[-1])
    tile = peak_end(1, 2, peak_sent, tile)
    level, inverse = levels(tile, 0.125)

    def saturated(values):
        return (level * jnp.tanh(values.astype(F32) * inverse)).astype(BF16)

    def piece_columns(k):
        first, count = PIECES[k]
        return slice(128 * first, 128 * (first + count))

    def saturate_piece(k):
        first, count = PIECES[k]
        if count == 1:
            for d in range(4):
                scaled_act[96 * d : 96 * d + 96, 768:896] = saturated(act1[d, 0:96, :])
            return
        for t in range(first, first + count):
            scaled_act[:, 128 * t : 128 * t + 128] = saturated(act[t])

    loads[2].wait()
    for at, k in enumerate(ended):
        act_y_end(k)
        saturate_piece(k)
        if at < len(ended) - 1:
            part = jnp.dot(
                scaled_act[:, piece_columns(k)], down_w[piece_columns(k), :],
                preferred_element_type=F32,
            )
            if at == 0:
                down_total[...] = part
            else:
                down_total[...] += part

    downs = [dict() for _ in range(3)]

    def down_multiply(n):
        columns = slice(256 * n, 256 * n + 256)
        last = piece_columns(ended[-1])
        result = down_total[:, columns] + jnp.dot(
            scaled_act[:, last], down_w[last, columns], preferred_element_type=F32
        )
        for half in range(2):
            for d in range(4):
                for c in range(2):
                    row = 96 * d + 48 * c
                    down_part[n, half, c, d] = result[row : row + 48, 128 * half : 128 * half + 128]
        core_send[n] = down_part[n, :, other].astype(BF16)
        downs[n]["core"] = send(core_send.at[n], core_recv.at[n], along("core", 1))

    def down_read(n, half, j):
        d = ring_add(j, x)
        return down_part[n, half, core, d] + core_recv[n, half, d].astype(F32)

    def down_x_first(n):
        downs[n]["core"].wait_recv()
        downs[n]["x"] = []
        for o in (2, 1, 3):
            for half in range(2):
                x_send[n, o - 1, half] = down_read(n, half, o).astype(BF16)
            downs[n]["x"].append(send(x_send.at[n, o - 1], x_recv.at[n, o - 1], along("x", o)))

    def down_l_first(n):
        for copy in downs[n]["x"]:
            copy.wait_recv()
        for half in range(2):
            total = down_read(n, half, 0) + sum(x_recv[n, o, half].astype(F32) for o in range(3))
            for i in range(4):
                rows = total if i == 0 else pltpu.roll(total, 48 - 12 * i, 0)
                l_own[n, i, half] = rows[0:16, :]
                l_send[n, i, half] = rows[0:16, :].astype(BF16)
        downs[n]["l"] = [
            send(l_send.at[n, ring_add(o, zl)], l_recv.at[n, o], along("zl", o)) for o in (1, 2, 3)
        ]

    def down_last(n):
        for copy in downs[n]["l"]:
            copy.wait_recv()
        for half in range(2):
            total = l_own[n, zl, half]
            for o in (1, 2, 3):
                total = total + l_recv[n, o, half].astype(F32)
            lanes = slice(256 * n + 128 * half, 256 * n + 128 * half + 128)
            out[:, lanes] = (token_pad[0:12, lanes] + total[0:12, :]).astype(BF16)

    for step, n in (
        (down_multiply, 0), (down_multiply, 1), (down_x_first, 0), (down_multiply, 2),
        (down_x_first, 1), (down_x_first, 2), (down_l_first, 0), (down_l_first, 1),
        (down_l_first, 2), (down_last, 0), (down_last, 1), (down_last, 2),
    ):
        step(n)

    for copy in copies:
        copy.wait_send()


def on_device(tokens, gate_weight, up_weight, down_weight):
    vmem = pltpu.VMEM
    return pl.pallas_call(
        kernel,
        out_shape=jax.ShapeDtypeStruct((12, 768), BF16),
        in_specs=[pl.BlockSpec(memory_space=pl.ANY)] * 4,
        out_specs=pl.BlockSpec(memory_space=pltpu.VMEM),
        scratch_shapes=[
            vmem((768, 896), BF16),
            vmem((768, 896), BF16),
            vmem((896, 768), BF16),
            vmem((12, 768), BF16),
            vmem((16, 768), F32),
            vmem((4, 16, 768), BF16),
            vmem((48, 768), F32),
            vmem((4, 2, 48, 768), BF16),
            vmem((384, 768), BF16),
            vmem((4, 7, 96, 128), F32),
            vmem((6, 7, 96, 128), BF16),
            vmem((6, 7, 96, 128), BF16),
            vmem((3, 2, 2, 96, 128), F32),
            vmem((2, 128, 128), F32),
            vmem((4, 3, 2, 48, 128), BF16),
            vmem((4, 3, 2, 48, 128), BF16),
            vmem((6, 384, 128), BF16),
            vmem((4, 128, 128), BF16),
            vmem((384, 896), BF16),
            vmem((384, 768), F32),
            vmem((3, 2, 2, 4, 48, 128), F32),
            vmem((3, 2, 4, 48, 128), BF16),
            vmem((3, 2, 4, 48, 128), BF16),
            vmem((3, 3, 2, 48, 128), BF16),
            vmem((3, 3, 2, 48, 128), BF16),
            vmem((3, 4, 2, 16, 128), F32),
            vmem((3, 4, 2, 16, 128), BF16),
            vmem((3, 4, 2, 16, 128), BF16),
            vmem((6, 1, 128), F32),
            vmem((6, 15, 1, 128), F32),
            pltpu.SemaphoreType.DMA((MAX_COPIES,)),
            pltpu.SemaphoreType.DMA((MAX_COPIES,)),
            pltpu.SemaphoreType.DMA((4,)),
        ],
        compiler_params=pltpu.CompilerParams(
            collective_id=0, has_side_effects=True, vmem_limit_bytes=60 * 1024 * 1024
        ),
        cost_estimate=pl.CostEstimate(
            flops=6 * 384 * 768 * 896, bytes_accessed=3 * 2 * 768 * 896, transcendentals=1000000
        ),
        name="swiglu_block",
    )(tokens, gate_weight, up_weight, down_weight)


def solution(mesh):
    in_specs = (
        P("hidden", "width"),
        P("width", "hidden"),
        P("width", "hidden"),
        P("hidden", "width"),
    )
    return jax.shard_map(
        on_device, mesh=mesh, in_specs=in_specs, out_specs=P("hidden", "width"), check_vma=False
    )
```

```python
import jax
import jax.numpy as jnp
from jax import lax
from jax.experimental import pallas as pl
from jax.experimental.pallas import tpu as pltpu
from jax.sharding import PartitionSpec as P

F32 = jnp.float32
BF16 = jnp.bfloat16

PIECES = ((6, 1), (0, 2), (2, 2), (4, 2))
Y_RING = (False, True, True, True)
Z_RING = (False, True, True, True)
STEPS = [(name[0], int(name[1])) for name in (
    "M1", "M0", "M2", "M3", "N1", "N2", "S1", "S2", "N3", "Y0",
    "S3", "Y1", "Y2", "P1", "Y3", "P2", "P3", "A0", "Z1", "Z2",
    "Z3", "A1", "A2", "A3",
)]
Z_ORDER = sorted(range(1, 16), key=lambda o: -min(o, 16 - o))
PLANE_ORDER = sorted(range(1, 16), key=lambda o: abs(o // 4 - 2) + abs(o % 4 - 2))
MAX_COPIES = 256


def ring_add(offset, value):
    return lax.rem(value + offset, 4)


def fold_max(values):
    rows, columns = values.shape
    total = None
    for row in range(0, rows, 8):
        for column in range(0, columns, 128):
            tile = jnp.abs(values[row : row + 8, column : column + 128])
            total = tile if total is None else jnp.maximum(total, tile)
    return jnp.max(total, axis=0, keepdims=True)


def levels(tile, factor):
    peak = jnp.max(tile, axis=1, keepdims=True)
    level = 0.5 * (factor * peak + 1e-06)
    return level, 1.0 / level


def kernel(
    tokens, gate_hbm, up_hbm, down_hbm, out,
    gate_w, up_w, down_w, token_in, token_pad, token_z, token_f, token_x, scaled,
    keep, y_send, y_recv, z_sum, z_sum1, z_send, z_recv, act, act1, scaled_act,
    down_total, down_part, core_send, core_recv, x_send, x_recv, l_own, l_send, l_recv,
    peak_send, peak_recv, send_sem, recv_sem, load_sem,
):
    width, hidden = lax.axis_index("width"), lax.axis_index("hidden")
    y, zh = lax.div(width, 4), lax.rem(width, 4)
    core = lax.rem(hidden, 2)
    x, zl = lax.div(hidden, 8), lax.rem(lax.div(hidden, 2), 4)
    other = 1 - core

    def device(y_=None, zh_=None, x_=None, zl_=None, core_=None):
        y_ = y if y_ is None else y_
        zh_ = zh if zh_ is None else zh_
        x_ = x if x_ is None else x_
        zl_ = zl if zl_ is None else zl_
        core_ = core if core_ is None else core_
        return (y_ * 4 + zh_, (x_ * 4 + zl_) * 2 + core_)

    def along(axis, offset):
        if axis == "y":
            return device(y_=ring_add(offset, y))
        if axis == "zh":
            return device(zh_=ring_add(offset, zh))
        if axis == "x":
            return device(x_=ring_add(offset, x))
        if axis == "zl":
            return device(zl_=ring_add(offset, zl))
        return device(core_=other)

    copies = []

    def send(source, target, to):
        at = len(copies)
        copy = pltpu.make_async_remote_copy(
            src_ref=source, dst_ref=target,
            send_sem=send_sem.at[at], recv_sem=recv_sem.at[at],
            device_id=to, device_id_type=pl.DeviceIdType.MESH,
        )
        copies.append(copy)
        copy.start()
        return copy

    loads = []
    for at, (source, target) in reversed(list(enumerate(
        ((gate_hbm, gate_w), (up_hbm, up_w), (down_hbm, down_w), (tokens, token_in))
    ))):
        load = pltpu.make_async_copy(source, target, load_sem.at[at])
        load.start()
        loads.insert(0, load)

    def z_partner(offset):
        z = lax.rem(zh * 4 + zl + offset, 16)
        return device(zh_=lax.div(z, 4), zl_=lax.rem(z, 4))

    def plane_partner(offset):
        return device(x_=ring_add(offset // 4, x), y_=ring_add(offset % 4, y))

    groups = (
        [along("core", 1)],
        [z_partner(o) for o in Z_ORDER],
        [plane_partner(o) for o in PLANE_ORDER],
    )
    partners = groups[1] + groups[2] + groups[0]
    barrier = pltpu.get_barrier_semaphore()
    for partner in partners:
        pl.semaphore_signal(barrier, inc=1, device_id=partner, device_id_type=pl.DeviceIdType.MESH)
    pl.semaphore_wait(barrier, len(partners))

    def peak_start(use, stage, tile):
        at = 3 * use + stage
        peak_send[at] = tile
        return [
            send(peak_send.at[at], peak_recv.at[at, o], to) for o, to in enumerate(groups[stage])
        ]

    def peak_end(use, stage, sent, tile):
        for o, copy in enumerate(sent):
            copy.wait_recv()
            tile = jnp.maximum(tile, peak_recv[3 * use + stage, o])
        return tile

    loads[3].wait()
    token_pad[0:12, :] = token_in[...].astype(F32)
    token_pad[12:16, :] = jnp.zeros((4, 768), F32)
    padded = token_pad[...]
    token_z[zl] = padded.astype(BF16)
    tile = fold_max(padded)
    peak_sent = peak_start(0, 0, tile)
    zl_sent = [send(token_z.at[zl], token_z.at[zl], along("zl", o)) for o in (1, 2, 3)]
    tile = peak_end(0, 0, peak_sent, tile)
    peak_sent = peak_start(0, 1, tile)
    for copy in zl_sent:
        copy.wait_recv()
    for i in range(4):
        token_f[12 * i : 12 * i + 12, :] = token_z[i].astype(F32)[0:12, :]
    token_x[x, core] = token_f[...].astype(BF16)
    mine = token_x.at[x, core]
    core_sent = [send(mine, mine, along("core", 1))]
    x_sent = [send(mine, mine, along("x", o)) for o in (1, 3, 2)]
    for o in (0, 1):
        x_sent[o].wait_recv()
        block = token_x.at[ring_add((3, 1)[o], x), core]
        core_sent.append(send(block, block, along("core", 1)))
    tile = peak_end(0, 1, peak_sent, tile)
    peak_sent = peak_start(0, 2, tile)
    x_sent[2].wait_recv()
    block = token_x.at[ring_add(2, x), core]
    core_sent.append(send(block, block, along("core", 1)))
    for copy in core_sent:
        copy.wait_recv()
    tile = peak_end(0, 2, peak_sent, tile)
    level, inverse = levels(tile, 1.0)
    for j in range(4):
        for c in range(2):
            values = token_x[ring_add(j, y), c].astype(F32)
            row = 96 * j + 48 * c
            scaled[row : row + 48, :] = (level * jnp.tanh(values * inverse)).astype(BF16)

    loads[0].wait()
    loads[1].wait()

    state = [dict() for _ in PIECES]

    def ring_sends(axis, which, sends, receives):
        ends = (along(axis, 1), along(axis, 3))
        return {m: send(sends(m), receives(m), ends[m % 2]) for m in which}

    def quarter(k, q):
        if PIECES[k][1] == 2:
            return lax.rem(q, 2), pl.multiple_of(lax.div(q, 2) * 48, 48), 48
        return 0, pl.multiple_of(q * 32, 32), 32

    def y_ring(k, which):
        tiles = pl.ds(*PIECES[k])
        return ring_sends("y", which, lambda m: y_send.at[m, tiles], lambda m: y_recv.at[m, tiles])

    def y_near(k):
        state[k]["y"].update(y_ring(k, (2, 3)))

    def z_ring(k, which):
        return ring_sends("zh", which, lambda m: z_slot(z_send, k, m), lambda m: z_slot(z_recv, k, m))

    def multiply(k):
        first, count = PIECES[k]
        columns = slice(128 * first, 128 * (first + count))
        gate = jnp.dot(scaled[...], gate_w[:, columns], preferred_element_type=F32)
        up = jnp.dot(scaled[...], up_w[:, columns], preferred_element_type=F32)
        tiles = pl.ds(first, count)
        for t in range(count):
            lanes = slice(128 * t, 128 * t + 128)
            if Y_RING[k]:
                y_send[0, first + t] = gate[192:288, lanes].astype(BF16)
                y_send[1, first + t] = up[192:288, lanes].astype(BF16)
                y_send[2, first + t] = up[96:192, lanes].astype(BF16)
                y_send[3, first + t] = gate[288:384, lanes].astype(BF16)
                keep[1, first + t] = gate[96:192, lanes]
                keep[3, first + t] = up[288:384, lanes]
            else:
                for o in range(3):
                    rows = slice(96 * o + 96, 96 * o + 192)
                    y_send[2 * o, first + t] = gate[rows, lanes].astype(BF16)
                    y_send[2 * o + 1, first + t] = up[rows, lanes].astype(BF16)
            keep[0, first + t] = gate[0:96, lanes]
            keep[2, first + t] = up[0:96, lanes]
        if Y_RING[k]:
            state[k]["y"] = y_ring(k, (0, 1))
        else:
            state[k]["y"] = [
                send(
                    y_send.at[pl.ds(2 * o - 2, 2), tiles],
                    y_recv.at[pl.ds(2 * o - 2, 2), tiles],
                    along("y", o),
                )
                for o in (2, 1, 3)
            ]

    def y_second(k):
        first, count = PIECES[k]
        for m, source, own in ((4, 0, 1), (5, 1, 3)):
            state[k]["y"][source].wait_recv()
            for t in range(first, first + count):
                y_send[m, t] = (keep[own, t] + y_recv[source, t].astype(F32)).astype(BF16)
            state[k]["y"].update(y_ring(k, (m,)))

    def z_read(k, g, q):
        tile_at, row, rows = quarter(k, q)
        if PIECES[k][1] == 2:
            return z_sum[PIECES[k][0] // 2, g, tile_at, pl.ds(row, rows), :]
        return z_sum1[g, pl.ds(row, rows), :]

    def z_rows(k):
        return quarter(k, 0)[2]

    def y_third(k):
        first, count = PIECES[k]
        ring = Y_RING[k]
        for m in (2, 3, 4, 5) if ring else range(3):
            state[k]["y"][m].wait_recv()
        for t in range(count):
            for g, arrived in ((0, (3, 4) if ring else (0, 2, 4)), (1, (2, 5) if ring else (1, 3, 5))):
                total = keep[2 * g, first + t]
                for m in arrived:
                    total = total + y_recv[m, first + t].astype(F32)
                if count == 2:
                    z_sum[PIECES[k][0] // 2, g, t] = total
                else:
                    z_sum1[g, 0:96, :] = total
        if count == 1:
            z_sum1[:, 96:128, :] = jnp.zeros((2, 32, 128), F32)
        rows = z_rows(k)
        if Z_RING[k]:
            for m in range(2):
                z_send[k, 0, m, 0:rows, :] = z_read(k, m, ring_add(2, zh)).astype(BF16)
            state[k]["z"] = z_ring(k, (0, 1))
            return
        state[k]["z"] = []
        for o in (2, 1, 3):
            for g in range(2):
                z_send[k, o - 1, g, 0:rows, :] = z_read(k, g, ring_add(o, zh)).astype(BF16)
            state[k]["z"].append(
                send(
                    z_send.at[k, o - 1, :, pl.ds(0, rows)],
                    z_recv.at[k, o - 1, :, pl.ds(0, rows)],
                    along("zh", o),
                )
            )

    def z_near(k):
        rows = z_rows(k)
        z_send[k, 1, 0, 0:rows, :] = z_read(k, 1, ring_add(1, zh)).astype(BF16)
        z_send[k, 1, 1, 0:rows, :] = z_read(k, 0, ring_add(3, zh)).astype(BF16)
        state[k]["z"].update(z_ring(k, (2, 3)))

    def z_slot(ref, k, m):
        return ref.at[k, m // 2, m % 2, pl.ds(0, z_rows(k))]

    def z_second(k):
        rows = z_rows(k)
        for m, g, j in ((4, 0, 1), (5, 1, 3)):
            state[k]["z"][m - 4].wait_recv()
            total = z_read(k, g, ring_add(j, zh)) + z_recv[k, 0, m - 4, 0:rows, :].astype(F32)
            z_send[k, 2, m - 4, 0:rows, :] = total.astype(BF16)
            state[k]["z"].update(z_ring(k, (m,)))

    def act_ref(k, owner_y, q):
        tile_at, row, rows = quarter(k, q)
        if PIECES[k][1] == 2:
            start = pl.multiple_of(owner_y * 96 + row, 16)
            return act.at[PIECES[k][0] + tile_at, pl.ds(start, rows), :]
        return act1.at[owner_y, pl.ds(row, rows), :]

    peaks = []

    def z_third(k):
        rows = z_rows(k)
        ring = Z_RING[k]
        for m in (2, 3, 4, 5) if ring else range(3):
            state[k]["z"][m].wait_recv()

        def summed(g, arrived):
            total = z_read(k, g, zh)
            for m in arrived:
                total = total + z_recv[k, m // 2, m % 2, 0:rows, :].astype(F32)
            return total

        gate = summed(0, (3, 4) if ring else (0, 2, 4))
        up = summed(1, (2, 5) if ring else (1, 3, 5))
        value = gate / (1.0 + jnp.exp(-gate)) * up
        peaks.append(fold_max(value))
        mine = act_ref(k, y, zh)
        mine[...] = value.astype(BF16)
        state[k]["az"] = {o: send(mine, mine, along("zh", o)) for o in (2, 1, 3)}
        state[k]["ay"] = []
        pass_on(k, 0)

    def pass_on(k, o):
        block = act_ref(k, y, ring_add(4 - o, zh))
        state[k]["ay"] += [send(block, block, along("y", place)) for place in (2, 1, 3)]

    def act_near(k):
        for o in (1, 3):
            state[k]["az"][o].wait_recv()
            pass_on(k, o)

    def act_far(k):
        state[k]["az"][2].wait_recv()
        pass_on(k, 2)

    def act_y_end(k):
        for copy in state[k]["ay"]:
            copy.wait_recv()

    def every(step, count=len(PIECES)):
        for k in range(count):
            step(k)

    for step, k in STEPS:
        {"M": multiply, "N": y_near, "P": z_near, "S": y_second, "Y": y_third, "Z": z_second, "A": z_third}[step](k)
    tile = peaks[0]
    for more in peaks[1:]:
        tile = jnp.maximum(tile, more)
    peak_sent = peak_start(1, 0, tile)
    ended = [k for step, k in STEPS if step == "A"]
    act_near(ended[0])
    tile = peak_end(1, 0, peak_sent, tile)
    peak_sent = peak_start(1, 1, tile)
    for k in ended[1:]:
        act_near(k)
    for k in ended[:-1]:
        act_far(k)
    tile = peak_end(1, 1, peak_sent, tile)
    peak_sent = peak_start(1, 2, tile)
    act_far(ended[-1])
    tile = peak_end(1, 2, peak_sent, tile)
    level, inverse = levels(tile, 0.125)

    def saturated(values):
        return (level * jnp.tanh(values.astype(F32) * inverse)).astype(BF16)

    def piece_columns(k):
        first, count = PIECES[k]
        return slice(128 * first, 128 * (first + count))

    def saturate_piece(k):
        first, count = PIECES[k]
        if count == 1:
            for d in range(4):
                scaled_act[96 * d : 96 * d + 96, 768:896] = saturated(act1[d, 0:96, :])
            return
        for t in range(first, first + count):
            scaled_act[:, 128 * t : 128 * t + 128] = saturated(act[t])

    loads[2].wait()
    for at, k in enumerate(ended):
        act_y_end(k)
        saturate_piece(k)
        if at < len(ended) - 1:
            part = jnp.dot(
                scaled_act[:, piece_columns(k)], down_w[piece_columns(k), :],
                preferred_element_type=F32,
            )
            if at == 0:
                down_total[...] = part
            else:
                down_total[...] += part

    downs = [dict() for _ in range(3)]

    def down_multiply(n):
        columns = slice(256 * n, 256 * n + 256)
        last = piece_columns(ended[-1])
        result = down_total[:, columns] + jnp.dot(
            scaled_act[:, last], down_w[last, columns], preferred_element_type=F32
        )
        for half in range(2):
            for d in range(4):
                for c in range(2):
                    row = 96 * d + 48 * c
                    down_part[n, half, c, d] = result[row : row + 48, 128 * half : 128 * half + 128]
        core_send[n] = down_part[n, :, other].astype(BF16)
        downs[n]["core"] = send(core_send.at[n], core_recv.at[n], along("core", 1))

    def down_read(n, half, j):
        d = ring_add(j, x)
        return down_part[n, half, core, d] + core_recv[n, half, d].astype(F32)

    def down_x_first(n):
        downs[n]["core"].wait_recv()
        downs[n]["x"] = []
        for o in (2, 1, 3):
            for half in range(2):
                x_send[n, o - 1, half] = down_read(n, half, o).astype(BF16)
            downs[n]["x"].append(send(x_send.at[n, o - 1], x_recv.at[n, o - 1], along("x", o)))

    def down_l_first(n):
        for copy in downs[n]["x"]:
            copy.wait_recv()
        for half in range(2):
            total = down_read(n, half, 0) + sum(x_recv[n, o, half].astype(F32) for o in range(3))
            for i in range(4):
                rows = total if i == 0 else pltpu.roll(total, 48 - 12 * i, 0)
                l_own[n, i, half] = rows[0:16, :]
                l_send[n, i, half] = rows[0:16, :].astype(BF16)
        downs[n]["l"] = [
            send(l_send.at[n, ring_add(o, zl)], l_recv.at[n, o], along("zl", o)) for o in (1, 2, 3)
        ]

    def down_last(n):
        for copy in downs[n]["l"]:
            copy.wait_recv()
        for half in range(2):
            total = l_own[n, zl, half]
            for o in (1, 2, 3):
                total = total + l_recv[n, o, half].astype(F32)
            lanes = slice(256 * n + 128 * half, 256 * n + 128 * half + 128)
            out[:, lanes] = (token_pad[0:12, lanes] + total[0:12, :]).astype(BF16)

    for step, n in (
        (down_multiply, 0), (down_multiply, 1), (down_x_first, 0), (down_multiply, 2),
        (down_x_first, 1), (down_x_first, 2), (down_l_first, 0), (down_l_first, 1),
        (down_l_first, 2), (down_last, 0), (down_last, 1), (down_last, 2),
    ):
        step(n)

    for copy in copies:
        copy.wait_send()


def on_device(tokens, gate_weight, up_weight, down_weight):
    vmem = pltpu.VMEM
    return pl.pallas_call(
        kernel,
        out_shape=jax.ShapeDtypeStruct((12, 768), BF16),
        in_specs=[pl.BlockSpec(memory_space=pl.ANY)] * 4,
        out_specs=pl.BlockSpec(memory_space=pltpu.VMEM),
        scratch_shapes=[
            vmem((768, 896), BF16),
            vmem((768, 896), BF16),
            vmem((896, 768), BF16),
            vmem((12, 768), BF16),
            vmem((16, 768), F32),
            vmem((4, 16, 768), BF16),
            vmem((48, 768), F32),
            vmem((4, 2, 48, 768), BF16),
            vmem((384, 768), BF16),
            vmem((4, 7, 96, 128), F32),
            vmem((6, 7, 96, 128), BF16),
            vmem((6, 7, 96, 128), BF16),
            vmem((3, 2, 2, 96, 128), F32),
            vmem((2, 128, 128), F32),
            vmem((4, 3, 2, 48, 128), BF16),
            vmem((4, 3, 2, 48, 128), BF16),
            vmem((6, 384, 128), BF16),
            vmem((4, 128, 128), BF16),
            vmem((384, 896), BF16),
            vmem((384, 768), F32),
            vmem((3, 2, 2, 4, 48, 128), F32),
            vmem((3, 2, 4, 48, 128), BF16),
            vmem((3, 2, 4, 48, 128), BF16),
            vmem((3, 3, 2, 48, 128), BF16),
            vmem((3, 3, 2, 48, 128), BF16),
            vmem((3, 4, 2, 16, 128), F32),
            vmem((3, 4, 2, 16, 128), BF16),
            vmem((3, 4, 2, 16, 128), BF16),
            vmem((6, 1, 128), F32),
            vmem((6, 15, 1, 128), F32),
            pltpu.SemaphoreType.DMA((MAX_COPIES,)),
            pltpu.SemaphoreType.DMA((MAX_COPIES,)),
            pltpu.SemaphoreType.DMA((4,)),
        ],
        compiler_params=pltpu.CompilerParams(
            collective_id=0, has_side_effects=True, vmem_limit_bytes=60 * 1024 * 1024
        ),
        cost_estimate=pl.CostEstimate(
            flops=6 * 384 * 768 * 896, bytes_accessed=3 * 2 * 768 * 896, transcendentals=1000000
        ),
        name="swiglu_block",
    )(tokens, gate_weight, up_weight, down_weight)


def solution(mesh):
    in_specs = (
        P("hidden", "width"),
        P("width", "hidden"),
        P("width", "hidden"),
        P("hidden", "width"),
    )
    return jax.shard_map(
        on_device, mesh=mesh, in_specs=in_specs, out_specs=P("hidden", "width"), check_vma=False
    )
```
